32 devices in a mesh: pool: 4 (over y, x), dev: 8 (over z, core).
Axes of the slice: x: 2, y: 2, z: 4, core: 2. Of those that a mesh axis runs over, the one named last changes fastest.
Arguments:
- patches: bfloat16 [64, 128, 1280], P('dev', 'pool'), may hold values from -6 to 6
- enc_tiles: int32 [8], replicated, may hold values from 1 to 8, 32 in all
- req_tiles: int32 [16], replicated, may hold values from 1 to 4, 32 in all
- req_owner: int32 [16, 1], replicated, may hold values from 0 to 3; in each aligned block of 16 rows (0 to 15, 16 to 31, ...) at most 6 rows name the same one
- fc1_weight: bfloat16 [1280, 5120], P(None, 'pool'), may hold values from -0.15625 to 0.15625
- fc2_weight: bfloat16 [5120, 1280], P('pool'), may hold values from -0.078125 to 0.078125
- key_weight: bfloat16 [1280, 1024], replicated, may hold values from -0.15625 to 0.15625
- value_weight: bfloat16 [1280, 1024], replicated, may hold values from -0.15625 to 0.15625
- query_weight: bfloat16 [8192, 8192], P(None, 'dev'), may hold values from -0.0625 to 0.0625
- out_weight: bfloat16 [8192, 8192], P('dev'), may hold values from -0.0625 to 0.0625
- text_hidden: bfloat16 [24, 4, 8192], P('pool'), may hold values from -6 to 6
Outputs:
- mixed: bfloat16 [24, 4, 8192], P('pool', None, 'dev')
The draws below stay inside these ranges and needn't reach their ends.
Inputs may be any that keep to these rules, and one draw needn't show every extreme that they name: `enc_tiles`: the entries sum to 32; the largest is 8. `req_tiles`: the entries sum to 32; the largest is 4. `req_owner`: no group owns more than 6 requests, and some group owns exactly 6.
All inputs are finite; a program needn't handle non-finite values.
Results may differ from the reference program's by a relative error of at most 0.008.
Values may be sent and summed in bfloat16 or wider, within the bound.
A program may use at most 128 MiB of HBM per device.

```python
import math
import jax
import jax.numpy as jnp
import numpy as np
from jax import lax

VW = 1280
VFF = 5120
D = 8192
HEADS = 64
KV_HEADS = 8
HEAD_DIM = 128
PT = 128
STEPS = 4
MAXT = 4
ENC_CAP = 8
TILES = 32
REQUESTS = 16
R_CAP = 6
N_POOL = 4
N_DEV = 8


def steps_of(key, shape, shards, smallest, top_value):
    factor_of, own = 1.0, jax.random.fold_in(key, 6)
    for dim, shards_of in shards:
        steps = jnp.exp(jax.random.uniform(jax.random.fold_in(own, dim), (shards_of,), jnp.float32, smallest / len(shards), top_value / len(shards)))
        factor_of = factor_of * jnp.repeat(steps, shape[dim] // shards_of).reshape([-1 if axis == dim else 1 for axis in range(len(shape))])
    return factor_of


def split_up(count, total, bound, lean):
    loads = [(1 << 20) // math.isqrt(rank ** lean) + 1 for rank in range(2, count + 1)]
    spare, holding = total - bound - (count - 1), [1] * (count - 1)
    while spare > 0:
        candidates = [i for i in range(count - 1) if holding[i] < bound]
        mass, remaining = sum([loads[i] for i in candidates]), spare
        for i in candidates:
            addition = min(bound - holding[i], max(1, remaining * loads[i] // mass), spare)
            holding[i] = holding[i] + addition
            spare = spare - addition
    return np.array([bound] + holding)


def ragged_sizes(rng, amount, total, limit, skew):
    if amount == 2:
        one = jax.random.randint(rng, (), max(1, total - limit), min(limit, total - 1) + 1)
        return jnp.stack([one, total - one])
    tallies = jnp.asarray(split_up(amount, total, limit, skew), jnp.int32)
    pairs = (amount - 1) // 2
    giver, taker = tallies[1:1 + 2 * pairs:2], tallies[2:2 + 2 * pairs:2]
    room = jnp.minimum(giver - 1, limit - taker)
    shifted = jax.random.randint(jax.random.fold_in(rng, 1), (pairs,), 0, 1 << 20) % (room + 1)
    tallies = tallies.at[1:1 + 2 * pairs:2].set(giver - shifted).at[2:2 + 2 * pairs:2].set(taker + shifted)
    return tallies[jax.random.permutation(jax.random.fold_in(rng, 2), amount)]


def routed_block(key, own, number, rows, number_of, top, bound, slope):
    order = jax.random.permutation(key, number_of)
    packed, common = load_shares(number_of, rows * top, bound, slope, True), load_shares(number_of, rows * top, bound, slope, False)
    places = jnp.arange(number_of)

    def named(sizes, offset_by):
        used = int((sizes > 0).sum())
        fixed = max(1, used // 4)
        passed = fixed + (places - fixed + offset_by * (used - fixed)) % max(1, number_of - fixed)
        return jnp.zeros((number_of,), jnp.int32).at[order[jnp.where(places < fixed, places, passed)]].set(jnp.asarray(sizes, jnp.int32))

    sizes = jnp.where(number % 4 == 0, named(packed, number // 4), named(common, number - number // 4 - 1))
    mixed = jax.random.permutation(jax.random.fold_in(own, 3), number_of)
    donor, sink = mixed[0:number_of // 2 * 2:2], mixed[1:number_of // 2 * 2:2]
    margin = jnp.minimum(sizes[donor] - 1, bound - sizes[sink]) // 2
    margin = jnp.where((donor == order[0]) | (sink == order[0]) | (sizes[sink] == 0), 0, jnp.maximum(margin, 0))
    passed = jax.random.randint(jax.random.fold_in(own, 4), (number_of // 2,), 0, 1 << 20) % (margin + 1)
    sizes = sizes.at[donor].add(-passed).at[sink].add(passed)
    members = jnp.searchsorted(jnp.cumsum(sizes), jnp.arange(rows * top), side="right").astype(jnp.int32)
    grid = members.reshape(top, rows).T
    grid = grid[jax.random.permutation(jax.random.fold_in(own, 1), rows)]
    offset_by = jax.random.randint(jax.random.fold_in(own, 2), (rows, 1), 0, top)
    return jnp.take_along_axis(grid, (jnp.arange(top)[None, :] + offset_by) % top, axis=1)


def load_shares(amount, total, reach, skew, full):
    weights = [(1 << 20) // math.isqrt(rank ** skew) + 1 for rank in range(1, amount + 1)]
    largest = reach if full else min(reach, max(-(-total // amount), total * weights[0] // sum(weights)))
    least = 1 if total - largest >= amount - 1 else 0
    holding, surplus = [largest] + [least] * (amount - 1), total - largest - least * (amount - 1)
    while surplus > 0:
        movable = [i for i in range(1, amount) if holding[i] < largest] or [i for i in range(1, amount) if holding[i] < reach]
        whole, budget = sum([weights[i] for i in movable]), surplus
        for i in movable:
            more = min(reach - holding[i], max(1, budget * weights[i] // whole), surplus)
            holding[i] = holding[i] + more
            surplus = surplus - more
    return np.array(holding)


def bell_draw(key, dims, scale, most, shards=(), kind=jnp.bfloat16):
    drawn = jax.random.normal(key, dims, jnp.float32) * scale
    if len(shards) > 0:
        drawn = steps_of(key, dims, shards, -0.22, 0.18) * drawn
    return jnp.clip(drawn, min=-most, max=most).astype(kind)


def setup_inputs(seed: int = 0) -> dict:
    streams_of = jax.random.split(jax.random.key(seed), 12)
    patches = bell_draw(streams_of[0], (N_DEV * ENC_CAP, PT, VW), 1.0, 6.0, ((0, 8), (1, 4)))
    enc_tiles = ragged_sizes(streams_of[1], N_DEV, TILES, ENC_CAP, 2).astype(jnp.int32)
    req_tiles = ragged_sizes(streams_of[2], REQUESTS, TILES, MAXT, 1).astype(jnp.int32)
    req_owner_keys = jax.random.split(jax.random.fold_in(streams_of[3], 1), REQUESTS // REQUESTS)
    req_owner_turns = jax.random.permutation(jax.random.fold_in(streams_of[3], 3), REQUESTS // REQUESTS)
    req_owner = jax.vmap(lambda own, number: routed_block(jax.random.fold_in(streams_of[3], 2), own, number, REQUESTS, N_POOL, 1, R_CAP, 1))(req_owner_keys, req_owner_turns).reshape((REQUESTS, 1))
    fc1_weight = bell_draw(streams_of[4], (VW, VFF), VW ** -0.5, 0.15625, ((1, 4),))
    fc2_weight = bell_draw(streams_of[5], (VFF, VW), VFF ** -0.5, 0.078125, ((0, 4),))
    key_weight = bell_draw(streams_of[6], (VW, KV_HEADS * HEAD_DIM), VW ** -0.5, 0.15625)
    value_weight = bell_draw(streams_of[7], (VW, KV_HEADS * HEAD_DIM), VW ** -0.5, 0.15625)
    query_weight = bell_draw(streams_of[8], (D, HEADS * HEAD_DIM), D ** -0.5, 0.0625, ((1, 8),))
    out_weight = bell_draw(streams_of[9], (HEADS * HEAD_DIM, D), (HEADS * HEAD_DIM) ** -0.5, 0.0625, ((0, 8),))
    text_hidden = bell_draw(streams_of[10], (N_POOL * R_CAP, STEPS, D), 1.0, 6.0, ((0, 4),))
    return {"patches": patches, "enc_tiles": enc_tiles, "req_tiles": req_tiles, "req_owner": req_owner, "fc1_weight": fc1_weight, "fc2_weight": fc2_weight, "key_weight": key_weight, "value_weight": value_weight, "query_weight": query_weight, "out_weight": out_weight, "text_hidden": text_hidden}


epsilon = 1e-05

def layer_stats(values_in):
    center = values_in - lax.optimization_barrier(jnp.mean(values_in, axis=-1, keepdims=True))
    spread = lax.optimization_barrier(jnp.mean(center * center, axis=-1, keepdims=True))
    return center / jnp.sqrt(spread + epsilon)

def rms_scale(values_in):
    return values_in / jnp.sqrt(lax.optimization_barrier(jnp.mean(values_in * values_in, axis=-1, keepdims=True)) + epsilon)

def slot_tables(enc_tiles, req_tiles, req_owner, groups, slots, capacity, most_tiles):
    enc_start = (jnp.cumsum(enc_tiles) - enc_tiles).astype(jnp.int32)
    req_start = (jnp.cumsum(req_tiles) - req_tiles).astype(jnp.int32)
    owner = req_owner[:, 0]
    group_ids = jnp.arange(groups, dtype=jnp.int32)
    member = (owner[:, None] == group_ids[None, :]).astype(jnp.int32)
    rank_in = lax.optimization_barrier(jnp.sum((jnp.cumsum(member, axis=0).astype(jnp.int32) - 1) * member, axis=1)).astype(jnp.int32)
    slot_ids = jnp.arange(slots, dtype=jnp.int32)
    match = ((owner[None, None, :] == group_ids[:, None, None]) & (rank_in[None, None, :] == slot_ids[None, :, None])).astype(jnp.int32)
    live = lax.optimization_barrier(jnp.sum(match, axis=2)) > 0
    length = lax.optimization_barrier(jnp.sum(match * req_tiles[None, None, :], axis=2)).astype(jnp.int32)
    first_tile = lax.optimization_barrier(jnp.sum(match * req_start[None, None, :], axis=2)).astype(jnp.int32)
    position = jnp.arange(most_tiles, dtype=jnp.int32)
    valid = position[None, None, :] < length[:, :, None]
    tile_index = first_tile[:, :, None] + position[None, None, :]
    column = (lax.optimization_barrier(jnp.sum((enc_start <= tile_index[..., None]).astype(jnp.int32), axis=-1)) - 1).astype(jnp.int32)
    column_hit = (column[..., None] == jnp.arange(enc_tiles.shape[0], dtype=jnp.int32)).astype(jnp.int32)
    column_start = lax.optimization_barrier(jnp.sum(column_hit * enc_start, axis=-1)).astype(jnp.int32)
    source = column * capacity + tile_index - column_start
    source = jnp.where(valid, source, 0).astype(jnp.int32)
    return (source, valid, live)

def reference(patches, enc_tiles, req_tiles, req_owner, fc1_weight, fc2_weight, key_weight, value_weight, query_weight, out_weight, text_hidden):
    columns = patches.reshape(N_DEV, ENC_CAP * PT, VW)

    def encode_column(column_rows):
        normed = layer_stats(column_rows.astype(jnp.float32)).astype(jnp.bfloat16)
        widened = jax.nn.gelu(jnp.dot(normed, fc1_weight, preferred_element_type=jnp.float32), approximate=False).astype(jnp.bfloat16)
        vision = (column_rows.astype(jnp.float32) + jnp.dot(widened, fc2_weight, preferred_element_type=jnp.float32)).astype(jnp.bfloat16)
        key_rows = rms_scale(jnp.dot(vision, key_weight, preferred_element_type=jnp.float32).reshape(ENC_CAP * PT, KV_HEADS, HEAD_DIM)).astype(jnp.bfloat16)
        value_rows = jnp.dot(vision, value_weight, preferred_element_type=jnp.float32).astype(jnp.bfloat16).reshape(ENC_CAP * PT, KV_HEADS, HEAD_DIM)
        return jnp.concatenate([key_rows, value_rows], axis=-1)
    kv_table = lax.map(encode_column, columns).reshape(N_DEV * ENC_CAP, PT, KV_HEADS, 2 * HEAD_DIM)
    source, valid, live = slot_tables(enc_tiles, req_tiles, req_owner, N_POOL, R_CAP, ENC_CAP, MAXT)
    scale = HEAD_DIM ** (-0.5)
    group_size = HEADS // KV_HEADS

    def decode_slot(inputs):
        hidden, slot_source, slot_valid, slot_live = inputs
        normed = rms_scale(hidden.astype(jnp.float32)).astype(jnp.bfloat16)
        query = jnp.dot(normed, query_weight, preferred_element_type=jnp.float32).reshape(STEPS, KV_HEADS, group_size, HEAD_DIM)
        query = rms_scale(query).astype(jnp.bfloat16)
        tiles = kv_table[slot_source]
        key_part = tiles[..., :HEAD_DIM].astype(jnp.float32)
        value_part = tiles[..., HEAD_DIM:].astype(jnp.float32)
        scores = jnp.einsum('sgqd,mngd->sgqmn', query.astype(jnp.float32), key_part) * scale
        weights = jnp.exp(scores) * slot_valid.astype(jnp.float32)[:, None]
        total = lax.optimization_barrier(jnp.sum(weights, axis=(3, 4)))
        total = jnp.where(slot_live, total, jnp.ones_like(total))
        weights = (weights / total[..., None, None]).astype(jnp.bfloat16)
        attended = jnp.einsum('sgqmn,mngd->sgqd', weights.astype(jnp.float32), value_part).astype(jnp.bfloat16)
        update = jnp.dot(attended.reshape(STEPS, HEADS * HEAD_DIM), out_weight, preferred_element_type=jnp.float32)
        return (hidden.astype(jnp.float32) + update).astype(jnp.bfloat16)
    return lax.map(decode_slot, (text_hidden, source.reshape(N_POOL * R_CAP, MAXT), valid.reshape(N_POOL * R_CAP, MAXT), live.reshape(N_POOL * R_CAP)))
```

```python
import jax
import jax.numpy as jnp
from jax import lax
from jax.experimental import pallas as pl
from jax.experimental.pallas import tpu as pltpu
from jax.sharding import PartitionSpec as P

MESH = pl.DeviceIdType.MESH

HEADS = 64
KV_HEADS = 8
HEAD_DIM = 128
MAXT = 4


epsilon = 1e-05


def layer_stats(values_in):
    center = values_in - jnp.mean(values_in, axis=-1, keepdims=True)
    spread = jnp.mean(center * center, axis=-1, keepdims=True)
    return center / jnp.sqrt(spread + epsilon)


def rms_scale(values_in):
    return values_in / jnp.sqrt(jnp.mean(values_in * values_in, axis=-1, keepdims=True) + epsilon)


def slot_tables(enc_tiles, req_tiles, req_owner, groups, slots, capacity, most_tiles):
    enc_start = jnp.cumsum(enc_tiles) - enc_tiles
    req_start = jnp.cumsum(req_tiles) - req_tiles
    owner = req_owner[:, 0]
    group_ids = jnp.arange(groups, dtype=jnp.int32)
    member = (owner[:, None] == group_ids[None, :]).astype(jnp.int32)
    rank_in = jnp.sum((jnp.cumsum(member, axis=0) - 1) * member, axis=1)
    slot_ids = jnp.arange(slots, dtype=jnp.int32)
    match = (
        (owner[None, None, :] == group_ids[:, None, None])
        & (rank_in[None, None, :] == slot_ids[None, :, None])
    ).astype(jnp.int32)
    live = jnp.sum(match, axis=2) > 0
    length = jnp.sum(match * req_tiles[None, None, :], axis=2)
    first_tile = jnp.sum(match * req_start[None, None, :], axis=2)
    position = jnp.arange(most_tiles, dtype=jnp.int32)
    valid = position[None, None, :] < length[:, :, None]
    tile_index = first_tile[:, :, None] + position[None, None, :]
    column = jnp.sum((enc_start <= tile_index[..., None]).astype(jnp.int32), axis=-1) - 1
    column_hit = (column[..., None] == jnp.arange(enc_tiles.shape[0], dtype=jnp.int32)).astype(
        jnp.int32
    )
    column_start = jnp.sum(column_hit * enc_start, axis=-1)
    source = column * capacity + tile_index - column_start
    source = jnp.where(valid, source, 0)
    return (source, valid, live)


def place_tiles(received, source, valid):
    flat_rows = received.reshape((received.shape[0] * received.shape[1],) + received.shape[2:])
    picked = jnp.take(flat_rows, source.reshape(-1), axis=0)
    picked = picked.reshape(source.shape + flat_rows.shape[1:])
    return jnp.where(valid[..., None, None], picked, jnp.zeros_like(picked))


def body(
    patches,
    enc_tiles,
    req_tiles,
    req_owner,
    fc1_weight,
    fc2_weight,
    key_weight,
    value_weight,
    query_weight,
    out_weight,
    text_hidden,
):
    capacity, quarter, width_in = patches.shape
    groups = lax.axis_size("pool")
    devices = lax.axis_size("dev")
    share_count = devices // KV_HEADS
    local_heads = HEADS // devices
    slots, steps, model_width = text_hidden.shape
    flat_patches = patches.reshape(capacity * quarter, width_in)
    normed = layer_stats(flat_patches.astype(jnp.float32)).astype(jnp.bfloat16)
    widened = jax.nn.gelu(
        jnp.dot(
            lax.all_gather(normed, "pool", axis=0, tiled=True),
            fc1_weight,
            preferred_element_type=jnp.float32,
        ),
        approximate=False,
    ).astype(jnp.bfloat16)
    update = lax.psum_scatter(
        jnp.dot(widened, fc2_weight, preferred_element_type=jnp.float32),
        "pool",
        scatter_dimension=0,
        tiled=True,
    )
    vision = (flat_patches.astype(jnp.float32) + update).astype(jnp.bfloat16)
    key_rows = rms_scale(
        jnp.dot(vision, key_weight, preferred_element_type=jnp.float32).reshape(
            capacity * quarter, KV_HEADS, HEAD_DIM
        )
    ).astype(jnp.bfloat16)
    value_rows = (
        jnp.dot(vision, value_weight, preferred_element_type=jnp.float32)
        .astype(jnp.bfloat16)
        .reshape(capacity * quarter, KV_HEADS, HEAD_DIM)
    )
    paired_rows = jnp.concatenate([key_rows, value_rows], axis=-1).reshape(
        capacity, quarter, KV_HEADS, 2 * HEAD_DIM
    )
    heads_first = jnp.transpose(paired_rows, (2, 0, 1, 3))
    source, valid, live = slot_tables(
        enc_tiles, req_tiles, req_owner, groups, slots, capacity, MAXT
    )
    copies_out = jnp.repeat(heads_first, share_count, axis=0)
    received = lax.all_to_all(copies_out, "dev", split_axis=0, concat_axis=0, tiled=True)
    arrived = lax.all_to_all(
        place_tiles(received, source, valid), "pool", split_axis=0, concat_axis=0, tiled=True
    )
    group_index = lax.axis_index("pool")
    slot_valid = lax.dynamic_index_in_dim(valid, group_index, 0, keepdims=False).astype(jnp.float32)
    slot_live = lax.dynamic_index_in_dim(live, group_index, 0, keepdims=False)
    normed_text = (
        rms_scale(text_hidden.astype(jnp.float32))
        .astype(jnp.bfloat16)
        .reshape(slots * steps, model_width)
    )
    query = jnp.dot(normed_text, query_weight, preferred_element_type=jnp.float32).reshape(
        slots, steps * local_heads, HEAD_DIM
    )
    query = rms_scale(query).astype(jnp.bfloat16)
    scores = jnp.einsum(
        "rad,prmnd->rapmn", query, arrived[..., :HEAD_DIM], preferred_element_type=jnp.float32
    ) * HEAD_DIM ** (-0.5)
    weights = jnp.exp(scores) * slot_valid[:, None, None, :, None]
    total = jnp.sum(weights, axis=(2, 3, 4))
    total = jnp.where(slot_live[:, None], total, jnp.ones_like(total))
    weights = (weights / total[:, :, None, None, None]).astype(jnp.bfloat16)
    attended = jnp.einsum(
        "rapmn,prmnd->rad", weights, arrived[..., HEAD_DIM:], preferred_element_type=jnp.float32
    ).astype(jnp.bfloat16)
    partial_out = jnp.dot(
        attended.reshape(slots * steps, local_heads * HEAD_DIM),
        out_weight,
        preferred_element_type=jnp.float32,
    )
    summed = lax.psum_scatter(
        partial_out.astype(jnp.bfloat16), "dev", scatter_dimension=1, tiled=True
    ).astype(jnp.float32)
    width_out = model_width // devices
    residual = lax.dynamic_slice_in_dim(
        text_hidden, lax.axis_index("dev") * width_out, width_out, 2
    )
    mixed = (residual.reshape(slots * steps, width_out).astype(jnp.float32) + summed).astype(
        jnp.bfloat16
    )
    return mixed.reshape(slots, steps, width_out)


def remote(source, target, send_sems, recv_sems, index, device):
    return pltpu.make_async_remote_copy(
        src_ref=source,
        dst_ref=target,
        send_sem=send_sems.at[index],
        recv_sem=recv_sems.at[index],
        device_id=device,
        device_id_type=MESH,
    )


def greet(pool_peers, dev_peers):
    barrier = pltpu.get_barrier_semaphore()
    for peer in pool_peers + dev_peers:
        pl.semaphore_signal(barrier, inc=1, device_id=peer, device_id_type=MESH)
    pl.semaphore_wait(barrier, len(pool_peers) + len(dev_peers))


def vision_kernel(
    patches_ref,
    text_ref,
    fc1_hbm,
    fc2_hbm,
    key_hbm,
    value_hbm,
    query_hbm,
    kv_out,
    query_out,
    fc1,
    fc2,
    key_map,
    value_map,
    query_map,
    rows,
    hidden,
    partial,
    own_sum,
    late_sum,
    outbox,
    diagonal_in,
    x_in,
    y_in,
    kv_box,
    kv_all,
    text_normed,
    query_sum,
    query_flat,
    query_all,
    local_sems,
    send_sems,
    recv_sems,
):
    pool, dev = lax.axis_index("pool"), lax.axis_index("dev")
    x, y = lax.rem(pool, 2), lax.div(pool, 2)
    x_peer = (y * 2 + 1 - x, dev)
    y_peer = ((1 - y) * 2 + x, dev)
    devices = kv_all.shape[0]
    chunks = rows.shape[0]
    part = rows.shape[1] // 4
    width = rows.shape[2]
    tile = 256

    loads = [
        pltpu.make_async_copy(fc1_hbm, fc1, local_sems.at[0]),
        pltpu.make_async_copy(fc2_hbm, fc2, local_sems.at[1]),
        pltpu.make_async_copy(key_hbm, key_map, local_sems.at[2]),
        pltpu.make_async_copy(value_hbm, value_map, local_sems.at[3]),
    ]
    pieces = query_map.shape[0]
    depth = query_map.shape[1]
    query_loads = [
        pltpu.make_async_copy(
            query_hbm.at[pl.ds(k * depth, depth), :], query_map.at[k], local_sems.at[4 + k]
        )
        for k in range(pieces)
    ]
    loads[0].start()
    loads[1].start()
    for load in query_loads:
        load.start()
    loads[2].start()
    loads[3].start()

    pool_peers = [(lax.rem(pool + k, 4), dev) for k in range(1, 4)]
    dev_peers = [(pool, lax.rem(dev + k, devices)) for k in range(1, devices)]
    greet(pool_peers, dev_peers)

    count = [0]

    def send(source, target, device):
        copy = remote(source, target, send_sems, recv_sems, count[0], device)
        count[0] += 1
        return copy

    def block(c, k):
        return rows.at[c, pl.ds(k * part, part)]

    to_x = [send(block(c, 0), block(c, 1), x_peer) for c in range(chunks)]
    to_y = [send(block(c, 0), block(c, 2), y_peer) for c in range(chunks)]
    half = chunks // 2
    onward = [
        send(block(c, 1), block(c, 3), y_peer)
        if c < half
        else send(block(c, 2), block(c, 3), x_peer)
        for c in range(chunks)
    ]

    def normalize(c):
        values = patches_ref[c * part : (c + 1) * part, :].astype(jnp.float32)
        rows[c, 0:part, :] = layer_stats(values).astype(jnp.bfloat16)

    for c in range(chunks):
        normalize(c)
        if c < half:
            to_x[c].start()
            to_y[c].start()

    text_normed[...] = rms_scale(text_ref[...].astype(jnp.float32))
    query_sum[...] = jnp.zeros_like(query_sum)

    def query_step(k):
        query_loads[k].wait()
        query_sum[...] += jnp.dot(
            text_normed[:, k * depth : (k + 1) * depth].astype(jnp.bfloat16),
            query_map[k],
            preferred_element_type=jnp.float32,
        )

    for c in range(half):
        query_step(2 * c)
        query_step(2 * c + 1)
        to_x[c].wait_recv()
        onward[c].start()
        to_x[half + c].start()
        to_y[half + c].start()
    for k in range(2 * half, pieces):
        query_step(k)
    text_rows = query_sum.shape[0]
    for h in range(query_sum.shape[1] // HEAD_DIM):
        query_flat[h * text_rows : (h + 1) * text_rows, :] = rms_scale(
            query_sum[:, h * HEAD_DIM : (h + 1) * HEAD_DIM]
        )
    query_all[pool] = query_flat[...].astype(jnp.bfloat16)
    query_sends = [send(query_all.at[pool], query_all.at[pool], peer) for peer in pool_peers]
    for copy in query_sends:
        copy.start()

    def feed_forward(c):
        def widen(n, carry):
            columns = pl.ds(pl.multiple_of(n * tile, tile), tile)
            pre = jnp.dot(rows[c], fc1[:, columns], preferred_element_type=jnp.float32)
            hidden[:, columns] = (0.5 * pre * (1.0 + lax.erf(pre * 0.7071067811865476))).astype(
                jnp.bfloat16
            )
            return carry

        def narrow(n, carry):
            columns = pl.ds(pl.multiple_of(n * tile, tile), tile)
            partial[:, columns] = jnp.dot(
                hidden[...], fc2[:, columns], preferred_element_type=jnp.float32
            )
            return carry

        lax.fori_loop(0, fc1.shape[1] // tile, widen, 0)
        lax.fori_loop(0, width // tile, narrow, 0)
        own_sum[c] = partial[0:part, :]
        late = 2 if c < half else 1
        late_sum[c] = partial[late * part : (late + 1) * part, :]
        early = 3 - late
        outbox[c, 0] = partial[3 * part : 4 * part, :].astype(jnp.bfloat16)
        outbox[c, 1] = partial[early * part : (early + 1) * part, :].astype(jnp.bfloat16)
        peer = x_peer if c < half else y_peer
        arrival = x_in if c < half else y_in
        copies = [
            send(outbox.at[c, 0], diagonal_in.at[c], peer),
            send(outbox.at[c, 1], arrival.at[c], peer),
        ]
        for copy in copies:
            copy.start()
        return copies

    def pass_on(c, copies):
        copies[0].wait_recv()
        outbox[c, 2] = (late_sum[c] + diagonal_in[c].astype(jnp.float32)).astype(jnp.bfloat16)
        peer = y_peer if c < half else x_peer
        arrival = y_in if c < half else x_in
        copy = send(outbox.at[c, 2], arrival.at[c], peer)
        copy.start()
        copies.append(copy)

    def project(c, copies):
        copies[1].wait_recv()
        copies[2].wait_recv()
        if c == 0:
            loads[2].wait()
            loads[3].wait()
        update = own_sum[c] + x_in[c].astype(jnp.float32) + y_in[c].astype(jnp.float32)
        vision = (
            patches_ref[c * part : (c + 1) * part, :].astype(jnp.float32) + update
        ).astype(jnp.bfloat16)
        pair = 2 * HEAD_DIM

        def two_heads(n, carry):
            columns = pl.ds(pl.multiple_of(n * pair, pair), pair)
            keys = jnp.dot(vision, key_map[:, columns], preferred_element_type=jnp.float32)
            values = jnp.dot(vision, value_map[:, columns], preferred_element_type=jnp.float32)
            for i in range(2):
                lanes = slice(i * HEAD_DIM, (i + 1) * HEAD_DIM)
                kv_box[c, 2 * n + i, :, 0:HEAD_DIM] = rms_scale(keys[:, lanes]).astype(jnp.bfloat16)
                kv_box[c, 2 * n + i, :, HEAD_DIM:pair] = values[:, lanes].astype(jnp.bfloat16)
            return carry

        lax.fori_loop(0, KV_HEADS // 2, two_heads, 0)
        kv_all[dev, c] = kv_box[c, dev]
        for peer in dev_peers:
            copy = send(kv_box.at[c, peer[1]], kv_all.at[dev, c], peer)
            copy.start()
            kv_sends.append(copy)

    kv_sends = []
    sums = [None] * chunks
    for c in range(half):
        to_y[c].wait_recv()
        onward[c].wait_recv()
        if c == 0:
            loads[0].wait()
            loads[1].wait()
        sums[c] = feed_forward(c)
        to_y[half + c].wait_recv()
        onward[half + c].start()
    pass_on(0, sums[0])
    for c in range(half, chunks):
        to_x[c].wait_recv()
        onward[c].wait_recv()
        sums[c] = feed_forward(c)
        pass_on(c - half + 1, sums[c - half + 1])
        project(c - half, sums[c - half])
    for c in range(half + 1, chunks):
        pass_on(c, sums[c])
    for c in range(half, chunks):
        project(c, sums[c])

    for copy in query_sends:
        copy.wait_recv()
    query_out[...] = query_all[...]
    for copy in kv_sends:
        copy.wait_recv()
    kv_out[...] = kv_all[...]
    for copy in to_x + to_y + onward + query_sends + kv_sends:
        copy.wait_send()
    for copies in sums:
        for copy in copies:
            copy.wait_send()


def decode_kernel(
    query_ref,
    kv_ref,
    member_ref,
    text_ref,
    out_hbm,
    mixed_ref,
    out_map,
    mask,
    gathered,
    outbox,
    inbox,
    attended,
    piece_out,
    piece_in,
    local_sems,
    send_sems,
    recv_sems,
):
    pool, dev = lax.axis_index("pool"), lax.axis_index("dev")
    devices = out_map.shape[0]
    width_out = out_map.shape[2]
    text_rows = text_ref.shape[0]
    order = list(range(1, devices)) + [0]
    loads = []
    for k in order:
        start = pl.multiple_of(lax.rem(dev + k, devices) * width_out, width_out)
        load = pltpu.make_async_copy(
            out_hbm.at[:, pl.ds(start, width_out)], out_map.at[k], local_sems.at[k]
        )
        load.start()
        loads.append(load)
    pool_peers = [(lax.rem(pool + k, 4), dev) for k in range(1, 4)]
    dev_peers = [(pool, lax.rem(dev + k, devices)) for k in range(1, devices)]
    greet(pool_peers, dev_peers)

    slots_all, keys_all = member_ref.shape[1], kv_ref.shape[0]
    quarter = keys_all // slots_all
    first = lax.broadcasted_iota(jnp.int32, (slots_all, keys_all), 0) * quarter
    column = lax.broadcasted_iota(jnp.int32, (slots_all, keys_all), 1)
    spread = jnp.where((column >= first) & (column < first + quarter), 1.0, 0.0).astype(
        jnp.bfloat16
    )
    for g in range(4):
        mask[g] = jnp.dot(
            member_ref[g * text_rows : (g + 1) * text_rows, :].astype(jnp.bfloat16),
            spread,
            preferred_element_type=jnp.float32,
        )

    span = 512
    heads = query_ref.shape[1] // text_rows

    def attend(group):
        gathered[...] = jnp.zeros_like(gathered)

        def step(b, carry):
            rows = pl.ds(pl.multiple_of(b * span, span), span)
            scores = lax.dot_general(
                query_ref[group],
                kv_ref[rows, 0:HEAD_DIM],
                (((1,), (1,)), ((), ())),
                preferred_element_type=jnp.float32,
            ) * HEAD_DIM ** (-0.5)
            weights = jnp.exp(scores).reshape(heads, text_rows, span) * mask[group, :, rows][None]
            values = jnp.concatenate(
                [kv_ref[rows, HEAD_DIM : 2 * HEAD_DIM], jnp.ones((span, HEAD_DIM), jnp.bfloat16)],
                axis=1,
            )
            gathered[...] += jnp.dot(
                weights.reshape(heads * text_rows, span).astype(jnp.bfloat16),
                values,
                preferred_element_type=jnp.float32,
            )
            return carry

        lax.fori_loop(0, keys_all // span, step, 0)

    lane = lax.broadcasted_iota(jnp.int32, (heads * text_rows, HEAD_DIM), 1)
    sends = []
    for k, peer in enumerate(pool_peers):
        attend(peer[0])
        total = gathered[:, HEAD_DIM : 2 * HEAD_DIM]
        coarse = total.astype(jnp.bfloat16).astype(jnp.float32)
        outbox[k, :, 0:HEAD_DIM] = gathered[:, 0:HEAD_DIM].astype(jnp.bfloat16)
        outbox[k, :, HEAD_DIM : 2 * HEAD_DIM] = jnp.where(
            lane < HEAD_DIM // 2, coarse, total - coarse
        ).astype(jnp.bfloat16)
        copy = remote(outbox.at[k], inbox.at[k], send_sems, recv_sems, k, peer)
        copy.start()
        sends.append(copy)
    attend(pool)
    for k, copy in enumerate(sends):
        copy.wait_recv()
        arrived = inbox[k].astype(jnp.float32)
        total = (
            arrived[:, HEAD_DIM : HEAD_DIM + 1]
            + arrived[:, HEAD_DIM + HEAD_DIM // 2 : HEAD_DIM + HEAD_DIM // 2 + 1]
        )
        gathered[:, 0:HEAD_DIM] += arrived[:, 0:HEAD_DIM]
        gathered[:, HEAD_DIM : 2 * HEAD_DIM] += jnp.broadcast_to(total, (total.shape[0], HEAD_DIM))
    total = gathered[:, HEAD_DIM : 2 * HEAD_DIM]
    result = gathered[:, 0:HEAD_DIM] / jnp.where(total > 0.0, total, 1.0)
    for h in range(heads):
        attended[:, h * HEAD_DIM : (h + 1) * HEAD_DIM] = result[
            h * text_rows : (h + 1) * text_rows, :
        ]
    left = attended[...].astype(jnp.bfloat16)
    half = width_out // 2
    copies = []
    for i, k in enumerate(order):
        loads[i].wait()
        product = jnp.dot(left, out_map[k], preferred_element_type=jnp.float32)
        if k > 0:
            piece_out[k - 1] = jnp.concatenate([product[:, :half], product[:, half:]], axis=0).astype(
                jnp.bfloat16
            )
            copy = remote(
                piece_out.at[k - 1], piece_in.at[k - 1], send_sems, recv_sems, 2 + k, dev_peers[k - 1]
            )
            copy.start()
            copies.append(copy)
    folded = jnp.concatenate([product[:, :half], product[:, half:]], axis=0)
    for k, copy in enumerate(copies):
        copy.wait_recv()
        folded = folded + piece_in[k].astype(jnp.float32)
    own = pl.ds(pl.multiple_of(dev * width_out, width_out), width_out)
    residual = text_ref[:, own].astype(jnp.float32)
    summed = jnp.concatenate([folded[:text_rows], folded[text_rows:]], axis=1)
    mixed_ref[...] = (residual + summed).astype(jnp.bfloat16)
    for copy in sends + copies:
        copy.wait_send()


def membership(enc_tiles, req_tiles, req_owner, groups, slots, steps, capacity):
    requests = req_tiles.shape[0]
    enc_start = jnp.cumsum(enc_tiles) - enc_tiles
    req_start = jnp.cumsum(req_tiles) - req_tiles
    owner = req_owner[:, 0]
    order = jnp.arange(requests, dtype=jnp.int32)
    earlier = (owner[:, None] == owner[None, :]) & (order[None, :] < order[:, None])
    rank = jnp.sum(earlier.astype(jnp.int32), axis=1)
    place = jnp.arange(capacity, dtype=jnp.int32)
    tile = (enc_start[:, None] + place[None, :]).reshape(-1)
    tile_live = (place[None, :] < enc_tiles[:, None]).reshape(-1)
    holds = (
        tile_live[None, :]
        & (tile[None, :] >= req_start[:, None])
        & (tile[None, :] < (req_start + req_tiles)[:, None])
    )
    slot = jnp.arange(groups * slots * steps, dtype=jnp.int32) // steps
    mine = slot[:, None] == (owner * slots + rank)[None, :]
    return jnp.any(mine[:, :, None] & holds[None, :, :], axis=1).astype(jnp.float32)


def fused_body(
    patches,
    enc_tiles,
    req_tiles,
    req_owner,
    fc1_weight,
    fc2_weight,
    key_weight,
    value_weight,
    query_weight,
    out_weight,
    text_hidden,
):
    capacity, quarter, width = patches.shape
    slots, steps, model_width = text_hidden.shape
    groups, devices = lax.axis_size("pool"), lax.axis_size("dev")
    local = query_weight.shape[1]
    heads = local // HEAD_DIM
    chunks = 4
    count = capacity * quarter
    part = count // chunks
    text_rows = slots * steps
    text = text_hidden.reshape(text_rows, model_width)
    vmem = pl.BlockSpec(memory_space=pltpu.VMEM)
    anywhere = pl.BlockSpec(memory_space=pl.ANY)
    bf16, f32 = jnp.bfloat16, jnp.float32
    pieces = 8
    copies = 6 * chunks + (groups - 1) + chunks * (devices - 1)
    kv, queries = pl.pallas_call(
        vision_kernel,
        out_shape=(
            jax.ShapeDtypeStruct((devices, chunks, part, 2 * HEAD_DIM), bf16),
            jax.ShapeDtypeStruct((groups, heads * text_rows, HEAD_DIM), bf16),
        ),
        in_specs=[vmem, vmem] + [anywhere] * 5,
        out_specs=(vmem, vmem),
        scratch_shapes=[
            pltpu.VMEM(fc1_weight.shape, bf16),
            pltpu.VMEM(fc2_weight.shape, bf16),
            pltpu.VMEM(key_weight.shape, bf16),
            pltpu.VMEM(value_weight.shape, bf16),
            pltpu.VMEM((pieces, model_width // pieces, local), bf16),
            pltpu.VMEM((chunks, 4 * part, width), bf16),
            pltpu.VMEM((4 * part, fc1_weight.shape[1]), bf16),
            pltpu.VMEM((4 * part, width), f32),
            pltpu.VMEM((chunks, part, width), f32),
            pltpu.VMEM((chunks, part, width), f32),
            pltpu.VMEM((chunks, 3, part, width), bf16),
            pltpu.VMEM((chunks, part, width), bf16),
            pltpu.VMEM((chunks, part, width), bf16),
            pltpu.VMEM((chunks, part, width), bf16),
            pltpu.VMEM((chunks, KV_HEADS, part, 2 * HEAD_DIM), bf16),
            pltpu.VMEM((devices, chunks, part, 2 * HEAD_DIM), bf16),
            pltpu.VMEM((text_rows, model_width), f32),
            pltpu.VMEM((text_rows, local), f32),
            pltpu.VMEM((heads * text_rows, HEAD_DIM), f32),
            pltpu.VMEM((groups, heads * text_rows, HEAD_DIM), bf16),
            pltpu.SemaphoreType.DMA((4 + pieces,)),
            pltpu.SemaphoreType.DMA((copies,)),
            pltpu.SemaphoreType.DMA((copies,)),
        ],
        compiler_params=pltpu.CompilerParams(
            collective_id=0, has_side_effects=True, vmem_limit_bytes=56 * 1024 * 1024
        ),
        name="vision",
    )(
        patches.reshape(count, width),
        text,
        fc1_weight,
        fc2_weight,
        key_weight,
        value_weight,
        query_weight,
    )
    member = membership(enc_tiles, req_tiles, req_owner, groups, slots, steps, capacity)
    width_out = model_width // devices
    piece = (devices - 1, 2 * text_rows, width_out // 2)
    mixed = pl.pallas_call(
        decode_kernel,
        out_shape=jax.ShapeDtypeStruct((text_rows, width_out), bf16),
        in_specs=[vmem] * 4 + [anywhere],
        out_specs=vmem,
        scratch_shapes=[
            pltpu.VMEM((devices, local, width_out), bf16),
            pltpu.VMEM((groups, text_rows, devices * count), f32),
            pltpu.VMEM((heads * text_rows, 2 * HEAD_DIM), f32),
            pltpu.VMEM((groups - 1, heads * text_rows, 2 * HEAD_DIM), bf16),
            pltpu.VMEM((groups - 1, heads * text_rows, 2 * HEAD_DIM), bf16),
            pltpu.VMEM((text_rows, local), f32),
            pltpu.VMEM(piece, bf16),
            pltpu.VMEM(piece, bf16),
            pltpu.SemaphoreType.DMA((devices,)),
            pltpu.SemaphoreType.DMA((devices + groups,)),
            pltpu.SemaphoreType.DMA((devices + groups,)),
        ],
        compiler_params=pltpu.CompilerParams(
            collective_id=1, has_side_effects=True, vmem_limit_bytes=48 * 1024 * 1024
        ),
        name="decode",
    )(queries, kv.reshape(devices * count, 2 * HEAD_DIM), member, text, out_weight)
    return mixed.reshape(slots, steps, width_out)


def solution(mesh):
    fits = mesh.shape["pool"] == 4 and mesh.shape["dev"] == KV_HEADS
    return jax.shard_map(
        fused_body if fits else body,
        mesh=mesh,
        in_specs=(
            P("dev", "pool", None),
            P(),
            P(),
            P(),
            P(None, "pool"),
            P("pool", None),
            P(),
            P(),
            P(None, "dev"),
            P("dev", None),
            P("pool", None, None),
        ),
        out_specs=P("pool", None, "dev"),
        check_vma=False,
    )
```

```python
import jax
import jax.numpy as jnp
from jax import lax
from jax.experimental import pallas as pl
from jax.experimental.pallas import tpu as pltpu
from jax.sharding import PartitionSpec as P

MESH = pl.DeviceIdType.MESH

HEADS = 64
KV_HEADS = 8
HEAD_DIM = 128
MAXT = 4


epsilon = 1e-05


def layer_stats(values_in):
    center = values_in - jnp.mean(values_in, axis=-1, keepdims=True)
    spread = jnp.mean(center * center, axis=-1, keepdims=True)
    return center / jnp.sqrt(spread + epsilon)


def rms_scale(values_in):
    return values_in / jnp.sqrt(jnp.mean(values_in * values_in, axis=-1, keepdims=True) + epsilon)


def slot_tables(enc_tiles, req_tiles, req_owner, groups, slots, capacity, most_tiles):
    enc_start = jnp.cumsum(enc_tiles) - enc_tiles
    req_start = jnp.cumsum(req_tiles) - req_tiles
    owner = req_owner[:, 0]
    group_ids = jnp.arange(groups, dtype=jnp.int32)
    member = (owner[:, None] == group_ids[None, :]).astype(jnp.int32)
    rank_in = jnp.sum((jnp.cumsum(member, axis=0) - 1) * member, axis=1)
    slot_ids = jnp.arange(slots, dtype=jnp.int32)
    match = (
        (owner[None, None, :] == group_ids[:, None, None])
        & (rank_in[None, None, :] == slot_ids[None, :, None])
    ).astype(jnp.int32)
    live = jnp.sum(match, axis=2) > 0
    length = jnp.sum(match * req_tiles[None, None, :], axis=2)
    first_tile = jnp.sum(match * req_start[None, None, :], axis=2)
    position = jnp.arange(most_tiles, dtype=jnp.int32)
    valid = position[None, None, :] < length[:, :, None]
    tile_index = first_tile[:, :, None] + position[None, None, :]
    column = jnp.sum((enc_start <= tile_index[..., None]).astype(jnp.int32), axis=-1) - 1
    column_hit = (column[..., None] == jnp.arange(enc_tiles.shape[0], dtype=jnp.int32)).astype(
        jnp.int32
    )
    column_start = jnp.sum(column_hit * enc_start, axis=-1)
    source = column * capacity + tile_index - column_start
    source = jnp.where(valid, source, 0)
    return (source, valid, live)


def place_tiles(received, source, valid):
    flat_rows = received.reshape((received.shape[0] * received.shape[1],) + received.shape[2:])
    picked = jnp.take(flat_rows, source.reshape(-1), axis=0)
    picked = picked.reshape(source.shape + flat_rows.shape[1:])
    return jnp.where(valid[..., None, None], picked, jnp.zeros_like(picked))


def body(
    patches,
    enc_tiles,
    req_tiles,
    req_owner,
    fc1_weight,
    fc2_weight,
    key_weight,
    value_weight,
    query_weight,
    out_weight,
    text_hidden,
):
    capacity, quarter, width_in = patches.shape
    groups = lax.axis_size("pool")
    devices = lax.axis_size("dev")
    share_count = devices // KV_HEADS
    local_heads = HEADS // devices
    slots, steps, model_width = text_hidden.shape
    flat_patches = patches.reshape(capacity * quarter, width_in)
    normed = layer_stats(flat_patches.astype(jnp.float32)).astype(jnp.bfloat16)
    widened = jax.nn.gelu(
        jnp.dot(
            lax.all_gather(normed, "pool", axis=0, tiled=True),
            fc1_weight,
            preferred_element_type=jnp.float32,
        ),
        approximate=False,
    ).astype(jnp.bfloat16)
    update = lax.psum_scatter(
        jnp.dot(widened, fc2_weight, preferred_element_type=jnp.float32),
        "pool",
        scatter_dimension=0,
        tiled=True,
    )
    vision = (flat_patches.astype(jnp.float32) + update).astype(jnp.bfloat16)
    key_rows = rms_scale(
        jnp.dot(vision, key_weight, preferred_element_type=jnp.float32).reshape(
            capacity * quarter, KV_HEADS, HEAD_DIM
        )
    ).astype(jnp.bfloat16)
    value_rows = (
        jnp.dot(vision, value_weight, preferred_element_type=jnp.float32)
        .astype(jnp.bfloat16)
        .reshape(capacity * quarter, KV_HEADS, HEAD_DIM)
    )
    paired_rows = jnp.concatenate([key_rows, value_rows], axis=-1).reshape(
        capacity, quarter, KV_HEADS, 2 * HEAD_DIM
    )
    heads_first = jnp.transpose(paired_rows, (2, 0, 1, 3))
    source, valid, live = slot_tables(
        enc_tiles, req_tiles, req_owner, groups, slots, capacity, MAXT
    )
    copies_out = jnp.repeat(heads_first, share_count, axis=0)
    received = lax.all_to_all(copies_out, "dev", split_axis=0, concat_axis=0, tiled=True)
    arrived = lax.all_to_all(
        place_tiles(received, source, valid), "pool", split_axis=0, concat_axis=0, tiled=True
    )
    group_index = lax.axis_index("pool")
    slot_valid = lax.dynamic_index_in_dim(valid, group_index, 0, keepdims=False).astype(jnp.float32)
    slot_live = lax.dynamic_index_in_dim(live, group_index, 0, keepdims=False)
    normed_text = (
        rms_scale(text_hidden.astype(jnp.float32))
        .astype(jnp.bfloat16)
        .reshape(slots * steps, model_width)
    )
    query = jnp.dot(normed_text, query_weight, preferred_element_type=jnp.float32).reshape(
        slots, steps * local_heads, HEAD_DIM
    )
    query = rms_scale(query).astype(jnp.bfloat16)
    scores = jnp.einsum(
        "rad,prmnd->rapmn", query, arrived[..., :HEAD_DIM], preferred_element_type=jnp.float32
    ) * HEAD_DIM ** (-0.5)
    weights = jnp.exp(scores) * slot_valid[:, None, None, :, None]
    total = jnp.sum(weights, axis=(2, 3, 4))
    total = jnp.where(slot_live[:, None], total, jnp.ones_like(total))
    weights = (weights / total[:, :, None, None, None]).astype(jnp.bfloat16)
    attended = jnp.einsum(
        "rapmn,prmnd->rad", weights, arrived[..., HEAD_DIM:], preferred_element_type=jnp.float32
    ).astype(jnp.bfloat16)
    partial_out = jnp.dot(
        attended.reshape(slots * steps, local_heads * HEAD_DIM),
        out_weight,
        preferred_element_type=jnp.float32,
    )
    summed = lax.psum_scatter(
        partial_out.astype(jnp.bfloat16), "dev", scatter_dimension=1, tiled=True
    ).astype(jnp.float32)
    width_out = model_width // devices
    residual = lax.dynamic_slice_in_dim(
        text_hidden, lax.axis_index("dev") * width_out, width_out, 2
    )
    mixed = (residual.reshape(slots * steps, width_out).astype(jnp.float32) + summed).astype(
        jnp.bfloat16
    )
    return mixed.reshape(slots, steps, width_out)


def remote(source, target, send_sems, recv_sems, index, device):
    return pltpu.make_async_remote_copy(
        src_ref=source,
        dst_ref=target,
        send_sem=send_sems.at[index],
        recv_sem=recv_sems.at[index],
        device_id=device,
        device_id_type=MESH,
    )


def greet(pool_peers, dev_peers):
    barrier = pltpu.get_barrier_semaphore()
    for peer in pool_peers + dev_peers:
        pl.semaphore_signal(barrier, inc=1, device_id=peer, device_id_type=MESH)
    pl.semaphore_wait(barrier, len(pool_peers) + len(dev_peers))


def block_kernel(
    enc_ref,
    tiles_ref,
    owner_ref,
    patches_ref,
    text_ref,
    fc1_hbm,
    fc2_hbm,
    key_hbm,
    value_hbm,
    query_hbm,
    out_hbm,
    mixed_ref,
    fc1,
    fc2,
    key_map,
    value_map,
    big_map,
    rows,
    hidden,
    partial,
    own_sum,
    late_sum,
    outbox,
    diagonal_in,
    x_in,
    y_in,
    kv_box,
    kv_all,
    text_raw,
    text_normed,
    query_sum,
    query_flat,
    query_all,
    mask,
    gathered,
    group_out,
    group_in,
    attended,
    piece_out,
    piece_in,
    local_sems,
    send_sems,
    recv_sems,
):
    pool, dev = lax.axis_index("pool"), lax.axis_index("dev")
    x, y = lax.rem(pool, 2), lax.div(pool, 2)
    x_peer = (y * 2 + 1 - x, dev)
    y_peer = ((1 - y) * 2 + x, dev)
    devices = kv_all.shape[1]
    chunks = rows.shape[0]
    part = rows.shape[1] // 4
    width = rows.shape[2]
    tile = 256
    slots, steps = text_ref.shape[0], text_ref.shape[1]
    text_rows = slots * steps
    pieces, depth, width_out = big_map.shape
    heads = query_sum.shape[1] // HEAD_DIM
    pair = 2 * HEAD_DIM
    tile_slots = 8

    loads = [
        pltpu.make_async_copy(fc1_hbm, fc1, local_sems.at[0]),
        pltpu.make_async_copy(fc2_hbm, fc2, local_sems.at[1]),
        pltpu.make_async_copy(key_hbm, key_map, local_sems.at[2]),
        pltpu.make_async_copy(value_hbm, value_map, local_sems.at[3]),
    ]
    query_loads = [
        pltpu.make_async_copy(
            query_hbm.at[pl.ds(k * depth, depth), :], big_map.at[k], local_sems.at[4 + k]
        )
        for k in range(pieces)
    ]
    out_loads = [
        pltpu.make_async_copy(
            out_hbm.at[
                :, pl.ds(pl.multiple_of(lax.rem(dev + k, devices) * width_out, width_out), width_out)
            ],
            big_map.at[k],
            local_sems.at[4 + pieces + k],
        )
        for k in range(devices)
    ]
    for load in query_loads[:4] + loads[:2] + query_loads[4:] + loads[2:]:
        load.start()

    pool_peers = [(lax.rem(pool + k, 4), dev) for k in range(1, 4)]
    dev_peers = [(pool, lax.rem(dev + k, devices)) for k in range(1, devices)]

    def normalize(c):
        values = patches_ref[c * part : (c + 1) * part, :].astype(jnp.float32)
        rows[c, 0:part, :] = layer_stats(values).astype(jnp.bfloat16)

    normalize(0)
    greet(pool_peers, dev_peers)

    count = [0]
    everything = []

    def send(source, target, device):
        copy = remote(source, target, send_sems, recv_sems, count[0], device)
        count[0] += 1
        everything.append(copy)
        return copy

    def block(c, k):
        return rows.at[c, pl.ds(k * part, part)]

    to_x = [send(block(c, 0), block(c, 1), x_peer) for c in range(chunks)]
    to_y = [send(block(c, 0), block(c, 2), y_peer) for c in range(chunks)]
    onward = [
        send(block(c, 1), block(c, 3), y_peer)
        if c % 2 == 0
        else send(block(c, 2), block(c, 3), x_peer)
        for c in range(chunks)
    ]

    def forward(c):
        first = to_x[c] if c % 2 == 0 else to_y[c]
        first.wait_recv()
        onward[c].start()

    def arrive(c):
        second = to_y[c] if c % 2 == 0 else to_x[c]
        second.wait_recv()
        onward[c].wait_recv()

    to_x[0].start()
    to_y[0].start()
    normalize(1)
    to_y[1].start()
    to_x[1].start()

    for s in range(slots):
        text_raw[s * steps : (s + 1) * steps, :] = text_ref[s].astype(jnp.float32)
    text_normed[...] = rms_scale(text_raw[...])
    query_sum[...] = jnp.zeros_like(query_sum)

    def query_step(k):
        query_loads[k].wait()
        query_sum[...] += jnp.dot(
            text_normed[:, k * depth : (k + 1) * depth].astype(jnp.bfloat16),
            big_map[k],
            preferred_element_type=jnp.float32,
        )

    for c in range(2, chunks):
        normalize(c)
    query_step(0)
    query_step(1)
    forward(0)
    forward(1)
    for c in range(2, chunks):
        to_x[c].start()
        to_y[c].start()
    for k in range(2, pieces):
        query_step(k)
    for load in out_loads[1:] + out_loads[:1]:
        load.start()
    for h in range(heads):
        query_flat[h * text_rows : (h + 1) * text_rows, :] = rms_scale(
            query_sum[:, h * HEAD_DIM : (h + 1) * HEAD_DIM]
        )
    query_all[pool] = query_flat[...].astype(jnp.bfloat16)
    query_sends = [send(query_all.at[pool], query_all.at[pool], peer) for peer in pool_peers]
    for copy in query_sends:
        copy.start()

    def tables():
        span = devices * part
        requests = tiles_ref.shape[0]
        quarter = part * chunks // tile_slots
        column = lax.broadcasted_iota(jnp.int32, (text_rows, span), 1)
        row_slot = lax.div(lax.broadcasted_iota(jnp.int32, (text_rows, span), 0), steps)
        source = lax.div(column, part)
        inner = lax.div(lax.rem(column, part), quarter)
        begin = jnp.zeros((text_rows, span), jnp.int32)
        size = jnp.zeros((text_rows, span), jnp.int32)
        running = 0
        for e in range(devices):
            begin = jnp.where(source == e, running, begin)
            size = jnp.where(source == e, enc_ref[e], size)
            running = running + enc_ref[e]
        owners = [owner_ref[r, 0] for r in range(requests)]
        names, starts, ends = [], [], []
        running = 0
        for r in range(requests):
            rank = 0
            for earlier in range(r):
                rank = rank + jnp.where(owners[earlier] == owners[r], 1, 0)
            names.append(owners[r] * slots + rank)
            starts.append(running)
            running = running + tiles_ref[r]
            ends.append(running)
        for c in range(chunks):
            place = inner + c * (part // quarter)
            index = begin + place
            name = jnp.full((text_rows, span), -1, jnp.int32)
            for r in range(requests):
                name = jnp.where((index >= starts[r]) & (index < ends[r]), names[r], name)
            name = jnp.where(place < size, name, -1)
            for g in range(4):
                mask[c, g] = jnp.where(row_slot + g * slots == name, 1.0, 0.0)

    tables()
    gathered[...] = jnp.zeros_like(gathered)

    def feed_forward(c):
        for n in range(fc1.shape[1] // tile):
            columns = slice(n * tile, (n + 1) * tile)
            pre = jnp.dot(rows[c], fc1[:, columns], preferred_element_type=jnp.float32)
            hidden[:, columns] = (0.5 * pre * (1.0 + lax.erf(pre * 0.7071067811865476))).astype(
                jnp.bfloat16
            )
        for n in range(width // tile):
            columns = slice(n * tile, (n + 1) * tile)
            partial[:, columns] = jnp.dot(
                hidden[...], fc2[:, columns], preferred_element_type=jnp.float32
            )
        late = 2 if c % 2 == 0 else 1
        early = 3 - late
        outbox[c, 0] = partial[3 * part : 4 * part, :].astype(jnp.bfloat16)
        peer = x_peer if c % 2 == 0 else y_peer
        arrival = x_in if c % 2 == 0 else y_in
        copies = [send(outbox.at[c, 0], diagonal_in.at[c], peer)]
        copies[0].start()
        outbox[c, 1] = partial[early * part : (early + 1) * part, :].astype(jnp.bfloat16)
        copies.append(send(outbox.at[c, 1], arrival.at[c], peer))
        copies[1].start()
        own_sum[c] = partial[0:part, :]
        late_sum[c] = partial[late * part : (late + 1) * part, :]
        sums[c] = copies

    def pass_on(c):
        sums[c][0].wait_recv()
        outbox[c, 2] = (late_sum[c] + diagonal_in[c].astype(jnp.float32)).astype(jnp.bfloat16)
        peer = y_peer if c % 2 == 0 else x_peer
        arrival = y_in if c % 2 == 0 else x_in
        copy = send(outbox.at[c, 2], arrival.at[c], peer)
        copy.start()
        sums[c].append(copy)

    def project(c):
        sums[c][1].wait_recv()
        sums[c][2].wait_recv()
        if c == 0:
            loads[2].wait()
            loads[3].wait()
        update = own_sum[c] + x_in[c].astype(jnp.float32) + y_in[c].astype(jnp.float32)
        vision = (
            patches_ref[c * part : (c + 1) * part, :].astype(jnp.float32) + update
        ).astype(jnp.bfloat16)
        for n in range(KV_HEADS // 2):
            columns = slice(n * pair, (n + 1) * pair)
            keys = jnp.dot(vision, key_map[:, columns], preferred_element_type=jnp.float32)
            values = jnp.dot(vision, value_map[:, columns], preferred_element_type=jnp.float32)
            for i in range(2):
                lanes = slice(i * HEAD_DIM, (i + 1) * HEAD_DIM)
                kv_box[c, 2 * n + i, :, 0:HEAD_DIM] = rms_scale(keys[:, lanes]).astype(jnp.bfloat16)
                kv_box[c, 2 * n + i, :, HEAD_DIM:pair] = values[:, lanes].astype(jnp.bfloat16)
        kv_all[c, dev] = kv_box[c, dev]
        kv_sends[c] = [
            send(kv_box.at[c, peer[1]], kv_all.at[c, dev], peer) for peer in dev_peers
        ]
        for copy in kv_sends[c]:
            copy.start()

    def attend(c, group):
        keys = kv_all[c, :, :, 0:HEAD_DIM].reshape(devices * part, HEAD_DIM)
        values = kv_all[c, :, :, HEAD_DIM:pair].reshape(devices * part, HEAD_DIM)
        scores = lax.dot_general(
            query_all[group], keys, (((1,), (1,)), ((), ())), preferred_element_type=jnp.float32
        ) * HEAD_DIM ** (-0.5)
        weights = (
            jnp.exp(scores).reshape(heads, text_rows, devices * part) * mask[c, group][None]
        )
        gathered[group] += jnp.dot(
            weights.reshape(heads * text_rows, devices * part).astype(jnp.bfloat16),
            jnp.concatenate([values, jnp.ones_like(values)], axis=1),
            preferred_element_type=jnp.float32,
        )

    def attend_all(c):
        for copy in kv_sends[c]:
            copy.wait_recv()

        def step(g, carry):
            attend(c, g)
            return carry

        lax.fori_loop(0, 4, step, 0)

    sums = [None] * chunks
    kv_sends = [None] * chunks
    loads[0].wait()
    loads[1].wait()
    arrive(0)
    feed_forward(0)
    forward(2)
    arrive(1)
    feed_forward(1)
    forward(3)
    pass_on(0)
    pass_on(1)
    arrive(2)
    feed_forward(2)
    project(0)
    arrive(3)
    feed_forward(3)
    pass_on(2)
    project(1)
    pass_on(3)
    for copy in query_sends:
        copy.wait_recv()
    attend_all(0)
    project(2)
    project(3)
    attend_all(1)
    attend_all(2)
    for copy in kv_sends[3]:
        copy.wait_recv()

    lane = lax.broadcasted_iota(jnp.int32, (heads * text_rows, HEAD_DIM), 1)
    group_sends = []
    for k, peer in enumerate(pool_peers):
        group = peer[0]
        attend(3, group)
        total = gathered[group, :, HEAD_DIM:pair]
        coarse = total.astype(jnp.bfloat16).astype(jnp.float32)
        group_out[k, :, 0:HEAD_DIM] = gathered[group, :, 0:HEAD_DIM].astype(jnp.bfloat16)
        group_out[k, :, HEAD_DIM:pair] = jnp.where(
            lane < HEAD_DIM // 2, coarse, total - coarse
        ).astype(jnp.bfloat16)
        copy = send(group_out.at[k], group_in.at[k], peer)
        copy.start()
        group_sends.append(copy)
    attend(3, pool)
    top = gathered[pool, :, 0:HEAD_DIM]
    total = gathered[pool, :, HEAD_DIM : HEAD_DIM + 1]
    middle = HEAD_DIM + HEAD_DIM // 2
    for k, copy in enumerate(group_sends):
        copy.wait_recv()
        arrived = group_in[k].astype(jnp.float32)
        top = top + arrived[:, 0:HEAD_DIM]
        total = total + (arrived[:, HEAD_DIM : HEAD_DIM + 1] + arrived[:, middle : middle + 1])
    result = top / jnp.where(total > 0.0, total, 1.0)
    for h in range(heads):
        attended[:, h * HEAD_DIM : (h + 1) * HEAD_DIM] = result[
            h * text_rows : (h + 1) * text_rows, :
        ]
    left = attended[...].astype(jnp.bfloat16)
    half = width_out // 2

    def piece(k):
        out_loads[k].wait()
        product = jnp.dot(left, big_map[k], preferred_element_type=jnp.float32)
        return jnp.concatenate([product[:, :half], product[:, half:]], axis=0)

    copies = []
    for k in range(1, devices):
        piece_out[k - 1] = piece(k).astype(jnp.bfloat16)
        copy = send(piece_out.at[k - 1], piece_in.at[k - 1], dev_peers[k - 1])
        copy.start()
        copies.append(copy)
    folded = piece(0)
    for k, copy in enumerate(copies):
        copy.wait_recv()
        folded = folded + piece_in[k].astype(jnp.float32)
    own = pl.ds(pl.multiple_of(dev * width_out, width_out), width_out)
    summed = jnp.concatenate([folded[:text_rows], folded[text_rows:]], axis=1)
    mixed = (text_raw[:, own] + summed).astype(jnp.bfloat16).astype(jnp.float32)
    for s in range(slots):
        mixed_ref[s] = mixed[s * steps : (s + 1) * steps, :].astype(jnp.bfloat16)
    for copy in everything:
        copy.wait_send()


def fused_body(
    patches,
    enc_tiles,
    req_tiles,
    req_owner,
    fc1_weight,
    fc2_weight,
    key_weight,
    value_weight,
    query_weight,
    out_weight,
    text_hidden,
):
    capacity, quarter, width = patches.shape
    slots, steps, model_width = text_hidden.shape
    groups, devices = lax.axis_size("pool"), lax.axis_size("dev")
    local = query_weight.shape[1]
    heads = local // HEAD_DIM
    chunks = 4
    count = capacity * quarter
    part = count // chunks
    text_rows = slots * steps
    vmem = pl.BlockSpec(memory_space=pltpu.VMEM)
    smem = pl.BlockSpec(memory_space=pltpu.SMEM)
    anywhere = pl.BlockSpec(memory_space=pl.ANY)
    bf16, f32 = jnp.bfloat16, jnp.float32
    width_out = model_width // devices
    pieces = model_width // width_out
    copies = 6 * chunks + 2 * (groups - 1) + (chunks + 1) * (devices - 1)
    group_box = (groups - 1, heads * text_rows, 2 * HEAD_DIM)
    piece = (devices - 1, 2 * text_rows, width_out // 2)
    return pl.pallas_call(
        block_kernel,
        out_shape=jax.ShapeDtypeStruct((slots, steps, width_out), bf16),
        in_specs=[smem] * 3 + [vmem] * 2 + [anywhere] * 6,
        out_specs=vmem,
        scratch_shapes=[
            pltpu.VMEM(fc1_weight.shape, bf16),
            pltpu.VMEM(fc2_weight.shape, bf16),
            pltpu.VMEM(key_weight.shape, bf16),
            pltpu.VMEM(value_weight.shape, bf16),
            pltpu.VMEM((pieces, local, width_out), bf16),
            pltpu.VMEM((chunks, 4 * part, width), bf16),
            pltpu.VMEM((4 * part, fc1_weight.shape[1]), bf16),
            pltpu.VMEM((4 * part, width), f32),
            pltpu.VMEM((chunks, part, width), f32),
            pltpu.VMEM((chunks, part, width), f32),
            pltpu.VMEM((chunks, 3, part, width), bf16),
            pltpu.VMEM((chunks, part, width), bf16),
            pltpu.VMEM((chunks, part, width), bf16),
            pltpu.VMEM((chunks, part, width), bf16),
            pltpu.VMEM((chunks, KV_HEADS, part, 2 * HEAD_DIM), bf16),
            pltpu.VMEM((chunks, devices, part, 2 * HEAD_DIM), bf16),
            pltpu.VMEM((text_rows, model_width), f32),
            pltpu.VMEM((text_rows, model_width), f32),
            pltpu.VMEM((text_rows, local), f32),
            pltpu.VMEM((heads * text_rows, HEAD_DIM), f32),
            pltpu.VMEM((groups, heads * text_rows, HEAD_DIM), bf16),
            pltpu.VMEM((chunks, groups, text_rows, devices * part), f32),
            pltpu.VMEM((groups, heads * text_rows, 2 * HEAD_DIM), f32),
            pltpu.VMEM(group_box, bf16),
            pltpu.VMEM(group_box, bf16),
            pltpu.VMEM((text_rows, local), f32),
            pltpu.VMEM(piece, bf16),
            pltpu.VMEM(piece, bf16),
            pltpu.SemaphoreType.DMA((4 + pieces + devices,)),
            pltpu.SemaphoreType.DMA((copies,)),
            pltpu.SemaphoreType.DMA((copies,)),
        ],
        compiler_params=pltpu.CompilerParams(
            collective_id=0, has_side_effects=True, vmem_limit_bytes=58 * 1024 * 1024
        ),
        name="block",
    )(
        enc_tiles,
        req_tiles,
        req_owner,
        patches.reshape(count, width),
        text_hidden,
        fc1_weight,
        fc2_weight,
        key_weight,
        value_weight,
        query_weight,
        out_weight,
    )


def solution(mesh):
    fits = mesh.shape["pool"] == 4 and mesh.shape["dev"] == KV_HEADS
    return jax.shard_map(
        fused_body if fits else body,
        mesh=mesh,
        in_specs=(
            P("dev", "pool", None),
            P(),
            P(),
            P(),
            P(None, "pool"),
            P("pool", None),
            P(),
            P(),
            P(None, "dev"),
            P("dev", None),
            P("pool", None, None),
        ),
        out_specs=P("pool", None, "dev"),
        check_vma=False,
    )
```

```python
import jax
import jax.numpy as jnp
from jax import lax
from jax.experimental import pallas as pl
from jax.experimental.pallas import tpu as pltpu
from jax.sharding import PartitionSpec as P

MESH = pl.DeviceIdType.MESH

HEADS = 64
KV_HEADS = 8
HEAD_DIM = 128
MAXT = 4


epsilon = 1e-05


def layer_stats(values_in):
    center = values_in - jnp.mean(values_in, axis=-1, keepdims=True)
    spread = jnp.mean(center * center, axis=-1, keepdims=True)
    return center / jnp.sqrt(spread + epsilon)


def rms_scale(values_in):
    return values_in / jnp.sqrt(jnp.mean(values_in * values_in, axis=-1, keepdims=True) + epsilon)


def slot_tables(enc_tiles, req_tiles, req_owner, groups, slots, capacity, most_tiles):
    enc_start = jnp.cumsum(enc_tiles) - enc_tiles
    req_start = jnp.cumsum(req_tiles) - req_tiles
    owner = req_owner[:, 0]
    group_ids = jnp.arange(groups, dtype=jnp.int32)
    member = (owner[:, None] == group_ids[None, :]).astype(jnp.int32)
    rank_in = jnp.sum((jnp.cumsum(member, axis=0) - 1) * member, axis=1)
    slot_ids = jnp.arange(slots, dtype=jnp.int32)
    match = (
        (owner[None, None, :] == group_ids[:, None, None])
        & (rank_in[None, None, :] == slot_ids[None, :, None])
    ).astype(jnp.int32)
    live = jnp.sum(match, axis=2) > 0
    length = jnp.sum(match * req_tiles[None, None, :], axis=2)
    first_tile = jnp.sum(match * req_start[None, None, :], axis=2)
    position = jnp.arange(most_tiles, dtype=jnp.int32)
    valid = position[None, None, :] < length[:, :, None]
    tile_index = first_tile[:, :, None] + position[None, None, :]
    column = jnp.sum((enc_start <= tile_index[..., None]).astype(jnp.int32), axis=-1) - 1
    column_hit = (column[..., None] == jnp.arange(enc_tiles.shape[0], dtype=jnp.int32)).astype(
        jnp.int32
    )
    column_start = jnp.sum(column_hit * enc_start, axis=-1)
    source = column * capacity + tile_index - column_start
    source = jnp.where(valid, source, 0)
    return (source, valid, live)


def place_tiles(received, source, valid):
    flat_rows = received.reshape((received.shape[0] * received.shape[1],) + received.shape[2:])
    picked = jnp.take(flat_rows, source.reshape(-1), axis=0)
    picked = picked.reshape(source.shape + flat_rows.shape[1:])
    return jnp.where(valid[..., None, None], picked, jnp.zeros_like(picked))


def body(
    patches,
    enc_tiles,
    req_tiles,
    req_owner,
    fc1_weight,
    fc2_weight,
    key_weight,
    value_weight,
    query_weight,
    out_weight,
    text_hidden,
):
    capacity, quarter, width_in = patches.shape
    groups = lax.axis_size("pool")
    devices = lax.axis_size("dev")
    share_count = devices // KV_HEADS
    local_heads = HEADS // devices
    slots, steps, model_width = text_hidden.shape
    flat_patches = patches.reshape(capacity * quarter, width_in)
    normed = layer_stats(flat_patches.astype(jnp.float32)).astype(jnp.bfloat16)
    widened = jax.nn.gelu(
        jnp.dot(
            lax.all_gather(normed, "pool", axis=0, tiled=True),
            fc1_weight,
            preferred_element_type=jnp.float32,
        ),
        approximate=False,
    ).astype(jnp.bfloat16)
    update = lax.psum_scatter(
        jnp.dot(widened, fc2_weight, preferred_element_type=jnp.float32),
        "pool",
        scatter_dimension=0,
        tiled=True,
    )
    vision = (flat_patches.astype(jnp.float32) + update).astype(jnp.bfloat16)
    key_rows = rms_scale(
        jnp.dot(vision, key_weight, preferred_element_type=jnp.float32).reshape(
            capacity * quarter, KV_HEADS, HEAD_DIM
        )
    ).astype(jnp.bfloat16)
    value_rows = (
        jnp.dot(vision, value_weight, preferred_element_type=jnp.float32)
        .astype(jnp.bfloat16)
        .reshape(capacity * quarter, KV_HEADS, HEAD_DIM)
    )
    paired_rows = jnp.concatenate([key_rows, value_rows], axis=-1).reshape(
        capacity, quarter, KV_HEADS, 2 * HEAD_DIM
    )
    heads_first = jnp.transpose(paired_rows, (2, 0, 1, 3))
    source, valid, live = slot_tables(
        enc_tiles, req_tiles, req_owner, groups, slots, capacity, MAXT
    )
    copies_out = jnp.repeat(heads_first, share_count, axis=0)
    received = lax.all_to_all(copies_out, "dev", split_axis=0, concat_axis=0, tiled=True)
    arrived = lax.all_to_all(
        place_tiles(received, source, valid), "pool", split_axis=0, concat_axis=0, tiled=True
    )
    group_index = lax.axis_index("pool")
    slot_valid = lax.dynamic_index_in_dim(valid, group_index, 0, keepdims=False).astype(jnp.float32)
    slot_live = lax.dynamic_index_in_dim(live, group_index, 0, keepdims=False)
    normed_text = (
        rms_scale(text_hidden.astype(jnp.float32))
        .astype(jnp.bfloat16)
        .reshape(slots * steps, model_width)
    )
    query = jnp.dot(normed_text, query_weight, preferred_element_type=jnp.float32).reshape(
        slots, steps * local_heads, HEAD_DIM
    )
    query = rms_scale(query).astype(jnp.bfloat16)
    scores = jnp.einsum(
        "rad,prmnd->rapmn", query, arrived[..., :HEAD_DIM], preferred_element_type=jnp.float32
    ) * HEAD_DIM ** (-0.5)
    weights = jnp.exp(scores) * slot_valid[:, None, None, :, None]
    total = jnp.sum(weights, axis=(2, 3, 4))
    total = jnp.where(slot_live[:, None], total, jnp.ones_like(total))
    weights = (weights / total[:, :, None, None, None]).astype(jnp.bfloat16)
    attended = jnp.einsum(
        "rapmn,prmnd->rad", weights, arrived[..., HEAD_DIM:], preferred_element_type=jnp.float32
    ).astype(jnp.bfloat16)
    partial_out = jnp.dot(
        attended.reshape(slots * steps, local_heads * HEAD_DIM),
        out_weight,
        preferred_element_type=jnp.float32,
    )
    summed = lax.psum_scatter(
        partial_out.astype(jnp.bfloat16), "dev", scatter_dimension=1, tiled=True
    ).astype(jnp.float32)
    width_out = model_width // devices
    residual = lax.dynamic_slice_in_dim(
        text_hidden, lax.axis_index("dev") * width_out, width_out, 2
    )
    mixed = (residual.reshape(slots * steps, width_out).astype(jnp.float32) + summed).astype(
        jnp.bfloat16
    )
    return mixed.reshape(slots, steps, width_out)


def center_rows(values_in):
    center = values_in - jnp.mean(values_in, axis=-1, keepdims=True)
    return center * lax.rsqrt(jnp.mean(center * center, axis=-1, keepdims=True) + epsilon)


def root_rows(values_in):
    return values_in * lax.rsqrt(
        jnp.mean(values_in * values_in, axis=-1, keepdims=True) + epsilon
    )


def remote(source, target, send_sems, recv_sems, index, device):
    return pltpu.make_async_remote_copy(
        src_ref=source,
        dst_ref=target,
        send_sem=send_sems.at[index],
        recv_sem=recv_sems.at[index],
        device_id=device,
        device_id_type=MESH,
    )


def greet(pool_peers, dev_peers):
    barrier = pltpu.get_barrier_semaphore()
    for peer in pool_peers + dev_peers:
        pl.semaphore_signal(barrier, inc=1, device_id=peer, device_id_type=MESH)
    pl.semaphore_wait(barrier, len(pool_peers) + len(dev_peers))


def block_kernel(
    enc_ref,
    tiles_ref,
    owner_ref,
    patches_ref,
    text_ref,
    fc1_hbm,
    fc2_hbm,
    key_hbm,
    value_hbm,
    query_hbm,
    out_hbm,
    mixed_ref,
    fc1,
    fc2,
    key_map,
    value_map,
    big_map,
    rows,
    hidden,
    own_sum,
    late_sum,
    outbox,
    diagonal_in,
    x_in,
    y_in,
    kv_box,
    kv_all,
    text_raw,
    text_normed,
    query_sum,
    query_flat,
    query_all,
    mask,
    gathered,
    group_out,
    group_in,
    attended,
    piece_out,
    piece_in,
    local_sems,
    send_sems,
    recv_sems,
):
    pool, dev = lax.axis_index("pool"), lax.axis_index("dev")
    x, y = lax.rem(pool, 2), lax.div(pool, 2)
    x_peer = (y * 2 + 1 - x, dev)
    y_peer = ((1 - y) * 2 + x, dev)
    devices = kv_all.shape[1]
    chunks = rows.shape[0]
    part = rows.shape[1] // 4
    width = rows.shape[2]
    tile = 256
    slots, steps = text_ref.shape[0], text_ref.shape[1]
    text_rows = slots * steps
    pieces, depth, width_out = big_map.shape
    heads = query_sum.shape[1] // HEAD_DIM
    pair = 2 * HEAD_DIM
    tile_slots = 8

    loads = [
        pltpu.make_async_copy(fc1_hbm, fc1, local_sems.at[0]),
        pltpu.make_async_copy(fc2_hbm, fc2, local_sems.at[1]),
        pltpu.make_async_copy(key_hbm, key_map, local_sems.at[2]),
        pltpu.make_async_copy(value_hbm, value_map, local_sems.at[3]),
    ]
    query_loads = [
        pltpu.make_async_copy(
            query_hbm.at[pl.ds(k * depth, depth), :], big_map.at[k], local_sems.at[4 + k]
        )
        for k in range(pieces)
    ]
    out_loads = [
        pltpu.make_async_copy(
            out_hbm.at[
                :, pl.ds(pl.multiple_of(lax.rem(dev + k, devices) * width_out, width_out), width_out)
            ],
            big_map.at[k],
            local_sems.at[4 + pieces + k],
        )
        for k in range(devices)
    ]
    for load in query_loads[:4] + loads[:2] + query_loads[4:] + loads[2:]:
        load.start()

    pool_peers = [(lax.rem(pool + k, 4), dev) for k in range(1, 4)]
    dev_peers = [(pool, lax.rem(dev + k, devices)) for k in range(1, devices)]

    def normalize(c):
        values = patches_ref[c * part : (c + 1) * part, :].astype(jnp.float32)
        rows[c, 0:part, :] = center_rows(values).astype(jnp.bfloat16)

    normalize(0)
    greet(pool_peers, dev_peers)

    count = [0]
    everything = []

    def send(source, target, device):
        copy = remote(source, target, send_sems, recv_sems, count[0], device)
        count[0] += 1
        everything.append(copy)
        return copy

    def block(c, k):
        return rows.at[c, pl.ds(k * part, part)]

    to_x = [send(block(c, 0), block(c, 1), x_peer) for c in range(chunks)]
    to_y = [send(block(c, 0), block(c, 2), y_peer) for c in range(chunks)]
    onward = [
        send(block(c, 1), block(c, 3), y_peer)
        if c % 2 == 0
        else send(block(c, 2), block(c, 3), x_peer)
        for c in range(chunks)
    ]

    def forward(c):
        first = to_x[c] if c % 2 == 0 else to_y[c]
        first.wait_recv()
        onward[c].start()

    def arrive(c):
        second = to_y[c] if c % 2 == 0 else to_x[c]
        second.wait_recv()
        onward[c].wait_recv()

    to_x[0].start()
    to_y[0].start()
    normalize(1)
    to_y[1].start()
    to_x[1].start()

    for s in range(slots):
        text_raw[s * steps : (s + 1) * steps, :] = text_ref[s].astype(jnp.float32)
    text_normed[...] = root_rows(text_raw[...])
    query_sum[...] = jnp.zeros_like(query_sum)

    def query_step(k):
        query_loads[k].wait()
        query_sum[...] += jnp.dot(
            text_normed[:, k * depth : (k + 1) * depth].astype(jnp.bfloat16),
            big_map[k],
            preferred_element_type=jnp.float32,
        )

    for c in range(2, chunks):
        normalize(c)
    query_step(0)
    query_step(1)
    forward(0)
    forward(1)
    for c in range(2, chunks):
        to_x[c].start()
        to_y[c].start()
    for k in range(2, pieces):
        query_step(k)
    for load in out_loads[1:] + out_loads[:1]:
        load.start()
    for h in range(heads):
        query_flat[h * text_rows : (h + 1) * text_rows, :] = root_rows(
            query_sum[:, h * HEAD_DIM : (h + 1) * HEAD_DIM]
        )
    query_all[pool] = query_flat[...].astype(jnp.bfloat16)
    query_sends = [send(query_all.at[pool], query_all.at[pool], peer) for peer in pool_peers]
    for copy in query_sends:
        copy.start()

    def tables():
        span = devices * part
        requests = tiles_ref.shape[0]
        quarter = part * chunks // tile_slots
        column = lax.broadcasted_iota(jnp.int32, (text_rows, span), 1)
        row_slot = lax.div(lax.broadcasted_iota(jnp.int32, (text_rows, span), 0), steps)
        source = lax.div(column, part)
        inner = lax.div(lax.rem(column, part), quarter)
        begin = jnp.zeros((text_rows, span), jnp.int32)
        size = jnp.zeros((text_rows, span), jnp.int32)
        running = 0
        for e in range(devices):
            begin = jnp.where(source == e, running, begin)
            size = jnp.where(source == e, enc_ref[e], size)
            running = running + enc_ref[e]
        owners = [owner_ref[r] for r in range(requests)]
        names, starts, ends = [], [], []
        running = 0
        for r in range(requests):
            rank = 0
            for earlier in range(r):
                rank = rank + jnp.where(owners[earlier] == owners[r], 1, 0)
            names.append(owners[r] * slots + rank)
            starts.append(running)
            running = running + tiles_ref[r]
            ends.append(running)
        for c in range(chunks):
            place = inner + c * (part // quarter)
            index = begin + place
            name = jnp.full((text_rows, span), -1, jnp.int32)
            for r in range(requests):
                name = jnp.where((index >= starts[r]) & (index < ends[r]), names[r], name)
            name = jnp.where(place < size, name, -1)
            for g in range(4):
                mask[c, g] = jnp.where(row_slot + g * slots == name, 1.0, 0.0)

    tables()

    def feed_forward(c):
        for n in range(fc1.shape[1] // tile):
            columns = slice(n * tile, (n + 1) * tile)
            pre = jnp.dot(rows[c], fc1[:, columns], preferred_element_type=jnp.float32)
            hidden[:, columns] = (0.5 * pre * (1.0 + lax.erf(pre * 0.7071067811865476))).astype(
                jnp.bfloat16
            )
        late = 2 if c % 2 == 0 else 1
        early = 3 - late
        for n in range(width // tile):
            columns = slice(n * tile, (n + 1) * tile)
            product = jnp.dot(hidden[...], fc2[:, columns], preferred_element_type=jnp.float32)
            outbox[c, 0, :, columns] = product[3 * part : 4 * part, :].astype(jnp.bfloat16)
            outbox[c, 1, :, columns] = product[early * part : (early + 1) * part, :].astype(
                jnp.bfloat16
            )
            own_sum[c, :, columns] = product[0:part, :]
            late_sum[c, :, columns] = product[late * part : (late + 1) * part, :]
        peer = x_peer if c % 2 == 0 else y_peer
        arrival = x_in if c % 2 == 0 else y_in
        copies = [
            send(outbox.at[c, 0], diagonal_in.at[c], peer),
            send(outbox.at[c, 1], arrival.at[c], peer),
        ]
        for copy in copies:
            copy.start()
        sums[c] = copies

    def pass_on(c):
        sums[c][0].wait_recv()
        outbox[c, 2] = (late_sum[c] + diagonal_in[c].astype(jnp.float32)).astype(jnp.bfloat16)
        peer = y_peer if c % 2 == 0 else x_peer
        arrival = y_in if c % 2 == 0 else x_in
        copy = send(outbox.at[c, 2], arrival.at[c], peer)
        copy.start()
        sums[c].append(copy)

    def project(*together):
        halves = []
        for c in together:
            sums[c][1].wait_recv()
            sums[c][2].wait_recv()
            update = own_sum[c] + x_in[c].astype(jnp.float32) + y_in[c].astype(jnp.float32)
            halves.append(patches_ref[c * part : (c + 1) * part, :].astype(jnp.float32) + update)
        if together[0] == 0:
            loads[2].wait()
            loads[3].wait()
        vision = jnp.concatenate(halves, axis=0).astype(jnp.bfloat16)
        for n in range(KV_HEADS // 2):
            columns = slice(n * pair, (n + 1) * pair)
            keys = jnp.dot(vision, key_map[:, columns], preferred_element_type=jnp.float32)
            values = jnp.dot(vision, value_map[:, columns], preferred_element_type=jnp.float32)
            for i in range(2):
                lanes = slice(i * HEAD_DIM, (i + 1) * HEAD_DIM)
                head_keys = root_rows(keys[:, lanes]).astype(jnp.bfloat16)
                head_values = values[:, lanes].astype(jnp.bfloat16)
                for t, c in enumerate(together):
                    span = slice(t * part, (t + 1) * part)
                    kv_box[c, 2 * n + i, :, 0:HEAD_DIM] = head_keys[span]
                    kv_box[c, 2 * n + i, :, HEAD_DIM:pair] = head_values[span]
        for c in together:
            kv_sends[c] = [
                send(kv_box.at[c, peer[1]], kv_all.at[c, dev], peer) for peer in dev_peers
            ]
            for copy in kv_sends[c]:
                copy.start()
            kv_all[c, dev] = kv_box[c, dev]

    def attend(c):
        for copy in kv_sends[c]:
            copy.wait_recv()
        keys = kv_all[c, :, :, 0:HEAD_DIM].reshape(devices * part, HEAD_DIM)
        values = kv_all[c, :, :, HEAD_DIM:pair].reshape(devices * part, HEAD_DIM)
        values = jnp.concatenate([values, jnp.ones_like(values)], axis=1)
        for g in range(4):
            scores = lax.dot_general(
                query_all[g], keys, (((1,), (1,)), ((), ())), preferred_element_type=jnp.float32
            )
            weights = jnp.exp2(scores * (HEAD_DIM ** (-0.5) * 1.4426950408889634)).reshape(
                heads, text_rows, devices * part
            ) * mask[c, g][None]
            added = jnp.dot(
                weights.reshape(heads * text_rows, devices * part).astype(jnp.bfloat16),
                values,
                preferred_element_type=jnp.float32,
            )
            gathered[g] = added if c == 0 else gathered[g] + added

    sums = [None] * chunks
    kv_sends = [None] * chunks
    loads[0].wait()
    loads[1].wait()
    arrive(0)
    feed_forward(0)
    forward(2)
    arrive(1)
    feed_forward(1)
    forward(3)
    pass_on(0)
    pass_on(1)
    arrive(2)
    feed_forward(2)
    arrive(3)
    feed_forward(3)
    pass_on(2)
    project(0, 1)
    pass_on(3)
    project(2)
    for copy in query_sends:
        copy.wait_recv()
    attend(0)
    project(3)
    attend(1)
    attend(2)
    attend(3)

    lane = lax.broadcasted_iota(jnp.int32, (heads * text_rows, HEAD_DIM), 1)
    group_sends = []
    for k, peer in enumerate(pool_peers):
        group = peer[0]
        total = gathered[group, :, HEAD_DIM:pair]
        coarse = total.astype(jnp.bfloat16).astype(jnp.float32)
        group_out[k, :, 0:HEAD_DIM] = gathered[group, :, 0:HEAD_DIM].astype(jnp.bfloat16)
        group_out[k, :, HEAD_DIM:pair] = jnp.where(
            lane < HEAD_DIM // 2, coarse, total - coarse
        ).astype(jnp.bfloat16)
        copy = send(group_out.at[k], group_in.at[k], peer)
        copy.start()
        group_sends.append(copy)
    top = gathered[pool, :, 0:HEAD_DIM]
    total = gathered[pool, :, HEAD_DIM : HEAD_DIM + 1]
    middle = HEAD_DIM + HEAD_DIM // 2
    for k, copy in enumerate(group_sends):
        copy.wait_recv()
        arrived = group_in[k].astype(jnp.float32)
        top = top + arrived[:, 0:HEAD_DIM]
        total = total + (arrived[:, HEAD_DIM : HEAD_DIM + 1] + arrived[:, middle : middle + 1])
    result = top / jnp.where(total > 0.0, total, 1.0)
    for h in range(heads):
        attended[:, h * HEAD_DIM : (h + 1) * HEAD_DIM] = result[
            h * text_rows : (h + 1) * text_rows, :
        ]
    left = attended[...].astype(jnp.bfloat16)
    half = width_out // 2

    def piece(k):
        out_loads[k].wait()
        product = jnp.dot(left, big_map[k], preferred_element_type=jnp.float32)
        return jnp.concatenate([product[:, :half], product[:, half:]], axis=0)

    copies = []
    for k in range(1, devices):
        piece_out[k - 1] = piece(k).astype(jnp.bfloat16)
        copy = send(piece_out.at[k - 1], piece_in.at[k - 1], dev_peers[k - 1])
        copy.start()
        copies.append(copy)
    folded = piece(0)
    for k, copy in enumerate(copies):
        copy.wait_recv()
        folded = folded + piece_in[k].astype(jnp.float32)
    own = pl.ds(pl.multiple_of(dev * width_out, width_out), width_out)
    summed = jnp.concatenate([folded[:text_rows], folded[text_rows:]], axis=1)
    mixed_ref[...] = (text_raw[:, own] + summed).astype(jnp.bfloat16)
    for copy in everything:
        copy.wait_send()


def fused_body(
    patches,
    enc_tiles,
    req_tiles,
    req_owner,
    fc1_weight,
    fc2_weight,
    key_weight,
    value_weight,
    query_weight,
    out_weight,
    text_hidden,
):
    capacity, quarter, width = patches.shape
    slots, steps, model_width = text_hidden.shape
    groups, devices = lax.axis_size("pool"), lax.axis_size("dev")
    local = query_weight.shape[1]
    heads = local // HEAD_DIM
    chunks = 4
    count = capacity * quarter
    part = count // chunks
    text_rows = slots * steps
    vmem = pl.BlockSpec(memory_space=pltpu.VMEM)
    smem = pl.BlockSpec(memory_space=pltpu.SMEM)
    anywhere = pl.BlockSpec(memory_space=pl.ANY)
    bf16, f32 = jnp.bfloat16, jnp.float32
    width_out = model_width // devices
    pieces = model_width // width_out
    copies = 6 * chunks + 2 * (groups - 1) + (chunks + 1) * (devices - 1)
    group_box = (groups - 1, heads * text_rows, 2 * HEAD_DIM)
    piece = (devices - 1, 2 * text_rows, width_out // 2)
    mixed = pl.pallas_call(
        block_kernel,
        out_shape=jax.ShapeDtypeStruct((text_rows, width_out), bf16),
        in_specs=[smem] * 3 + [vmem] * 2 + [anywhere] * 6,
        out_specs=vmem,
        scratch_shapes=[
            pltpu.VMEM(fc1_weight.shape, bf16),
            pltpu.VMEM(fc2_weight.shape, bf16),
            pltpu.VMEM(key_weight.shape, bf16),
            pltpu.VMEM(value_weight.shape, bf16),
            pltpu.VMEM((pieces, local, width_out), bf16),
            pltpu.VMEM((chunks, 4 * part, width), bf16),
            pltpu.VMEM((4 * part, fc1_weight.shape[1]), bf16),
            pltpu.VMEM((chunks, part, width), f32),
            pltpu.VMEM((chunks, part, width), f32),
            pltpu.VMEM((chunks, 3, part, width), bf16),
            pltpu.VMEM((chunks, part, width), bf16),
            pltpu.VMEM((chunks, part, width), bf16),
            pltpu.VMEM((chunks, part, width), bf16),
            pltpu.VMEM((chunks, KV_HEADS, part, 2 * HEAD_DIM), bf16),
            pltpu.VMEM((chunks, devices, part, 2 * HEAD_DIM), bf16),
            pltpu.VMEM((text_rows, model_width), f32),
            pltpu.VMEM((text_rows, model_width), f32),
            pltpu.VMEM((text_rows, local), f32),
            pltpu.VMEM((heads * text_rows, HEAD_DIM), f32),
            pltpu.VMEM((groups, heads * text_rows, HEAD_DIM), bf16),
            pltpu.VMEM((chunks, groups, text_rows, devices * part), f32),
            pltpu.VMEM((groups, heads * text_rows, 2 * HEAD_DIM), f32),
            pltpu.VMEM(group_box, bf16),
            pltpu.VMEM(group_box, bf16),
            pltpu.VMEM((text_rows, local), f32),
            pltpu.VMEM(piece, bf16),
            pltpu.VMEM(piece, bf16),
            pltpu.SemaphoreType.DMA((4 + pieces + devices,)),
            pltpu.SemaphoreType.DMA((copies,)),
            pltpu.SemaphoreType.DMA((copies,)),
        ],
        compiler_params=pltpu.CompilerParams(
            collective_id=0, has_side_effects=True, vmem_limit_bytes=58 * 1024 * 1024
        ),
        name="block",
    )(
        enc_tiles,
        req_tiles,
        req_owner.reshape(-1),
        patches.reshape(count, width),
        text_hidden,
        fc1_weight,
        fc2_weight,
        key_weight,
        value_weight,
        query_weight,
        out_weight,
    )
    return mixed.reshape(slots, steps, width_out)


def solution(mesh):
    fits = mesh.shape["pool"] == 4 and mesh.shape["dev"] == KV_HEADS
    return jax.shard_map(
        fused_body if fits else body,
        mesh=mesh,
        in_specs=(
            P("dev", "pool", None),
            P(),
            P(),
            P(),
            P(None, "pool"),
            P("pool", None),
            P(),
            P(),
            P(None, "dev"),
            P("dev", None),
            P("pool", None, None),
        ),
        out_specs=P("pool", None, "dev"),
        check_vma=False,
    )
```

```python
import jax
import jax.numpy as jnp
from jax import lax
from jax.experimental import pallas as pl
from jax.experimental.pallas import tpu as pltpu
from jax.sharding import PartitionSpec as P

MESH = pl.DeviceIdType.MESH

HEADS = 64
KV_HEADS = 8
HEAD_DIM = 128
MAXT = 4


epsilon = 1e-05


def layer_stats(values_in):
    center = values_in - jnp.mean(values_in, axis=-1, keepdims=True)
    spread = jnp.mean(center * center, axis=-1, keepdims=True)
    return center / jnp.sqrt(spread + epsilon)


def rms_scale(values_in):
    return values_in / jnp.sqrt(jnp.mean(values_in * values_in, axis=-1, keepdims=True) + epsilon)


def slot_tables(enc_tiles, req_tiles, req_owner, groups, slots, capacity, most_tiles):
    enc_start = jnp.cumsum(enc_tiles) - enc_tiles
    req_start = jnp.cumsum(req_tiles) - req_tiles
    owner = req_owner[:, 0]
    group_ids = jnp.arange(groups, dtype=jnp.int32)
    member = (owner[:, None] == group_ids[None, :]).astype(jnp.int32)
    rank_in = jnp.sum((jnp.cumsum(member, axis=0) - 1) * member, axis=1)
    slot_ids = jnp.arange(slots, dtype=jnp.int32)
    match = (
        (owner[None, None, :] == group_ids[:, None, None])
        & (rank_in[None, None, :] == slot_ids[None, :, None])
    ).astype(jnp.int32)
    live = jnp.sum(match, axis=2) > 0
    length = jnp.sum(match * req_tiles[None, None, :], axis=2)
    first_tile = jnp.sum(match * req_start[None, None, :], axis=2)
    position = jnp.arange(most_tiles, dtype=jnp.int32)
    valid = position[None, None, :] < length[:, :, None]
    tile_index = first_tile[:, :, None] + position[None, None, :]
    column = jnp.sum((enc_start <= tile_index[..., None]).astype(jnp.int32), axis=-1) - 1
    column_hit = (column[..., None] == jnp.arange(enc_tiles.shape[0], dtype=jnp.int32)).astype(
        jnp.int32
    )
    column_start = jnp.sum(column_hit * enc_start, axis=-1)
    source = column * capacity + tile_index - column_start
    source = jnp.where(valid, source, 0)
    return (source, valid, live)


def place_tiles(received, source, valid):
    flat_rows = received.reshape((received.shape[0] * received.shape[1],) + received.shape[2:])
    picked = jnp.take(flat_rows, source.reshape(-1), axis=0)
    picked = picked.reshape(source.shape + flat_rows.shape[1:])
    return jnp.where(valid[..., None, None], picked, jnp.zeros_like(picked))


def body(
    patches,
    enc_tiles,
    req_tiles,
    req_owner,
    fc1_weight,
    fc2_weight,
    key_weight,
    value_weight,
    query_weight,
    out_weight,
    text_hidden,
):
    capacity, quarter, width_in = patches.shape
    groups = lax.axis_size("pool")
    devices = lax.axis_size("dev")
    share_count = devices // KV_HEADS
    local_heads = HEADS // devices
    slots, steps, model_width = text_hidden.shape
    flat_patches = patches.reshape(capacity * quarter, width_in)
    normed = layer_stats(flat_patches.astype(jnp.float32)).astype(jnp.bfloat16)
    widened = jax.nn.gelu(
        jnp.dot(
            lax.all_gather(normed, "pool", axis=0, tiled=True),
            fc1_weight,
            preferred_element_type=jnp.float32,
        ),
        approximate=False,
    ).astype(jnp.bfloat16)
    update = lax.psum_scatter(
        jnp.dot(widened, fc2_weight, preferred_element_type=jnp.float32),
        "pool",
        scatter_dimension=0,
        tiled=True,
    )
    vision = (flat_patches.astype(jnp.float32) + update).astype(jnp.bfloat16)
    key_rows = rms_scale(
        jnp.dot(vision, key_weight, preferred_element_type=jnp.float32).reshape(
            capacity * quarter, KV_HEADS, HEAD_DIM
        )
    ).astype(jnp.bfloat16)
    value_rows = (
        jnp.dot(vision, value_weight, preferred_element_type=jnp.float32)
        .astype(jnp.bfloat16)
        .reshape(capacity * quarter, KV_HEADS, HEAD_DIM)
    )
    paired_rows = jnp.concatenate([key_rows, value_rows], axis=-1).reshape(
        capacity, quarter, KV_HEADS, 2 * HEAD_DIM
    )
    heads_first = jnp.transpose(paired_rows, (2, 0, 1, 3))
    source, valid, live = slot_tables(
        enc_tiles, req_tiles, req_owner, groups, slots, capacity, MAXT
    )
    copies_out = jnp.repeat(heads_first, share_count, axis=0)
    received = lax.all_to_all(copies_out, "dev", split_axis=0, concat_axis=0, tiled=True)
    arrived = lax.all_to_all(
        place_tiles(received, source, valid), "pool", split_axis=0, concat_axis=0, tiled=True
    )
    group_index = lax.axis_index("pool")
    slot_valid = lax.dynamic_index_in_dim(valid, group_index, 0, keepdims=False).astype(jnp.float32)
    slot_live = lax.dynamic_index_in_dim(live, group_index, 0, keepdims=False)
    normed_text = (
        rms_scale(text_hidden.astype(jnp.float32))
        .astype(jnp.bfloat16)
        .reshape(slots * steps, model_width)
    )
    query = jnp.dot(normed_text, query_weight, preferred_element_type=jnp.float32).reshape(
        slots, steps * local_heads, HEAD_DIM
    )
    query = rms_scale(query).astype(jnp.bfloat16)
    scores = jnp.einsum(
        "rad,prmnd->rapmn", query, arrived[..., :HEAD_DIM], preferred_element_type=jnp.float32
    ) * HEAD_DIM ** (-0.5)
    weights = jnp.exp(scores) * slot_valid[:, None, None, :, None]
    total = jnp.sum(weights, axis=(2, 3, 4))
    total = jnp.where(slot_live[:, None], total, jnp.ones_like(total))
    weights = (weights / total[:, :, None, None, None]).astype(jnp.bfloat16)
    attended = jnp.einsum(
        "rapmn,prmnd->rad", weights, arrived[..., HEAD_DIM:], preferred_element_type=jnp.float32
    ).astype(jnp.bfloat16)
    partial_out = jnp.dot(
        attended.reshape(slots * steps, local_heads * HEAD_DIM),
        out_weight,
        preferred_element_type=jnp.float32,
    )
    summed = lax.psum_scatter(
        partial_out.astype(jnp.bfloat16), "dev", scatter_dimension=1, tiled=True
    ).astype(jnp.float32)
    width_out = model_width // devices
    residual = lax.dynamic_slice_in_dim(
        text_hidden, lax.axis_index("dev") * width_out, width_out, 2
    )
    mixed = (residual.reshape(slots * steps, width_out).astype(jnp.float32) + summed).astype(
        jnp.bfloat16
    )
    return mixed.reshape(slots, steps, width_out)


def center_rows(values_in):
    center = values_in - jnp.mean(values_in, axis=-1, keepdims=True)
    return center * lax.rsqrt(jnp.mean(center * center, axis=-1, keepdims=True) + epsilon)


def root_rows(values_in):
    return values_in * lax.rsqrt(
        jnp.mean(values_in * values_in, axis=-1, keepdims=True) + epsilon
    )


def remote(source, target, send_sems, recv_sems, index, device):
    return pltpu.make_async_remote_copy(
        src_ref=source,
        dst_ref=target,
        send_sem=send_sems.at[index],
        recv_sem=recv_sems.at[index],
        device_id=device,
        device_id_type=MESH,
    )


def greet(pool_peers, dev_peers):
    barrier = pltpu.get_barrier_semaphore()
    for peer in pool_peers + dev_peers:
        pl.semaphore_signal(barrier, inc=1, device_id=peer, device_id_type=MESH)
    pl.semaphore_wait(barrier, len(pool_peers) + len(dev_peers))


def block_kernel(
    enc_ref,
    tiles_ref,
    owner_ref,
    patches_ref,
    text_ref,
    fc1_hbm,
    fc2_hbm,
    key_hbm,
    value_hbm,
    query_hbm,
    out_hbm,
    mixed_ref,
    fc1,
    fc2,
    key_map,
    value_map,
    big_map,
    rows,
    hidden,
    own_sum,
    late_sum,
    outbox,
    diagonal_in,
    x_in,
    y_in,
    kv_box,
    kv_all,
    text_raw,
    text_normed,
    query_sum,
    query_flat,
    query_all,
    mask,
    gathered,
    group_out,
    group_in,
    total_out,
    total_in,
    attended,
    pair_out,
    pair_in,
    piece_out,
    piece_in,
    local_sems,
    send_sems,
    recv_sems,
):
    pool, dev = lax.axis_index("pool"), lax.axis_index("dev")
    x, y = lax.rem(pool, 2), lax.div(pool, 2)
    x_peer = (y * 2 + 1 - x, dev)
    y_peer = ((1 - y) * 2 + x, dev)
    devices = kv_all.shape[1]
    chunks = rows.shape[0]
    part = rows.shape[1] // 4
    width = rows.shape[2]
    tile = 256
    slots, steps = text_ref.shape[0], text_ref.shape[1]
    text_rows = slots * steps
    pieces, depth, width_out = big_map.shape
    heads = query_sum.shape[1] // HEAD_DIM
    pair = 2 * HEAD_DIM
    tile_slots = 8

    loads = [
        pltpu.make_async_copy(fc1_hbm, fc1, local_sems.at[0]),
        pltpu.make_async_copy(fc2_hbm, fc2, local_sems.at[1]),
        pltpu.make_async_copy(key_hbm, key_map, local_sems.at[2]),
        pltpu.make_async_copy(value_hbm, value_map, local_sems.at[3]),
    ]
    query_loads = [
        pltpu.make_async_copy(
            query_hbm.at[pl.ds(k * depth, depth), :], big_map.at[k], local_sems.at[4 + k]
        )
        for k in range(pieces)
    ]
    chips = devices // 2
    chip, core = lax.div(dev, 2), lax.rem(dev, 2)
    ahead = [lax.rem(chip + k, chips) for k in list(range(1, chips)) + [0]]
    targets = [place * 2 + 1 - core for place in ahead] + [place * 2 + core for place in ahead]
    partner = (pool, chip * 2 + 1 - core)
    out_loads = [
        pltpu.make_async_copy(
            out_hbm.at[:, pl.ds(pl.multiple_of(target * width_out, width_out), width_out)],
            big_map.at[k],
            local_sems.at[4 + pieces + k],
        )
        for k, target in enumerate(targets)
    ]
    for load in query_loads[:4] + loads[:2] + query_loads[4:] + loads[2:]:
        load.start()

    pool_peers = [(lax.rem(pool + k, 4), dev) for k in range(1, 4)]
    dev_peers = [(pool, lax.rem(dev + k, devices)) for k in range(1, devices)]

    def normalize(c):
        values = patches_ref[c * part : (c + 1) * part, :].astype(jnp.float32)
        rows[c, 0:part, :] = center_rows(values).astype(jnp.bfloat16)

    normalize(0)
    greet(pool_peers, dev_peers)

    count = [0]
    everything = []

    def send(source, target, device):
        copy = remote(source, target, send_sems, recv_sems, count[0], device)
        count[0] += 1
        everything.append(copy)
        return copy

    def block(c, k):
        return rows.at[c, pl.ds(k * part, part)]

    to_x = [send(block(c, 0), block(c, 1), x_peer) for c in range(chunks)]
    to_y = [send(block(c, 0), block(c, 2), y_peer) for c in range(chunks)]
    onward = [
        send(block(c, 1), block(c, 3), y_peer)
        if c % 2 == 0
        else send(block(c, 2), block(c, 3), x_peer)
        for c in range(chunks)
    ]

    def forward(c):
        first = to_x[c] if c % 2 == 0 else to_y[c]
        first.wait_recv()
        onward[c].start()

    def arrive(c):
        second = to_y[c] if c % 2 == 0 else to_x[c]
        second.wait_recv()
        onward[c].wait_recv()

    to_x[0].start()
    to_y[0].start()
    normalize(1)
    to_y[1].start()
    to_x[1].start()

    for s in range(slots):
        text_raw[s * steps : (s + 1) * steps, :] = text_ref[s].astype(jnp.float32)
    text_normed[...] = root_rows(text_raw[...])
    query_sum[...] = jnp.zeros_like(query_sum)

    def query_step(k):
        query_loads[k].wait()
        query_sum[...] += jnp.dot(
            text_normed[:, k * depth : (k + 1) * depth].astype(jnp.bfloat16),
            big_map[k],
            preferred_element_type=jnp.float32,
        )

    for c in range(2, chunks):
        normalize(c)
    query_step(0)
    query_step(1)
    forward(0)
    forward(1)
    for c in range(2, chunks):
        to_x[c].start()
        to_y[c].start()
    for k in range(2, pieces):
        query_step(k)
    for load in out_loads:
        load.start()
    for h in range(heads):
        query_flat[h * text_rows : (h + 1) * text_rows, :] = root_rows(
            query_sum[:, h * HEAD_DIM : (h + 1) * HEAD_DIM]
        )
    query_all[pool] = query_flat[...].astype(jnp.bfloat16)
    query_sends = [send(query_all.at[pool], query_all.at[pool], peer) for peer in pool_peers]
    for copy in query_sends:
        copy.start()

    def tables():
        span = devices * part
        requests = tiles_ref.shape[0]
        quarter = part * chunks // tile_slots
        column = lax.broadcasted_iota(jnp.int32, (text_rows, span), 1)
        row_slot = lax.div(lax.broadcasted_iota(jnp.int32, (text_rows, span), 0), steps)
        source = lax.div(column, part)
        inner = lax.div(lax.rem(column, part), quarter)
        begin = jnp.zeros((text_rows, span), jnp.int32)
        size = jnp.zeros((text_rows, span), jnp.int32)
        running = 0
        for e in range(devices):
            begin = jnp.where(source == e, running, begin)
            size = jnp.where(source == e, enc_ref[e], size)
            running = running + enc_ref[e]
        owners = [owner_ref[r] for r in range(requests)]
        names, starts, ends = [], [], []
        running = 0
        for r in range(requests):
            rank = 0
            for earlier in range(r):
                rank = rank + jnp.where(owners[earlier] == owners[r], 1, 0)
            names.append(owners[r] * slots + rank)
            starts.append(running)
            running = running + tiles_ref[r]
            ends.append(running)
        for c in range(chunks):
            place = inner + c * (part // quarter)
            index = begin + place
            name = jnp.full((text_rows, span), -1, jnp.int32)
            for r in range(requests):
                name = jnp.where((index >= starts[r]) & (index < ends[r]), names[r], name)
            name = jnp.where(place < size, name, -1)
            for g in range(4):
                mask[c, g] = jnp.where(row_slot + g * slots == name, 1.0, 0.0)

    tables()

    def feed_forward(c):
        for n in range(fc1.shape[1] // tile):
            columns = slice(n * tile, (n + 1) * tile)
            pre = jnp.dot(rows[c], fc1[:, columns], preferred_element_type=jnp.float32)
            hidden[:, columns] = (0.5 * pre * (1.0 + lax.erf(pre * 0.7071067811865476))).astype(
                jnp.bfloat16
            )
        late = 2 if c % 2 == 0 else 1
        early = 3 - late
        for n in range(width // tile):
            columns = slice(n * tile, (n + 1) * tile)
            product = jnp.dot(hidden[...], fc2[:, columns], preferred_element_type=jnp.float32)
            outbox[c, 0, :, columns] = product[3 * part : 4 * part, :].astype(jnp.bfloat16)
            outbox[c, 1, :, columns] = product[early * part : (early + 1) * part, :].astype(
                jnp.bfloat16
            )
            own_sum[c, :, columns] = product[0:part, :]
            late_sum[c, :, columns] = product[late * part : (late + 1) * part, :]
        peer = x_peer if c % 2 == 0 else y_peer
        arrival = x_in if c % 2 == 0 else y_in
        copies = [
            send(outbox.at[c, 0], diagonal_in.at[c], peer),
            send(outbox.at[c, 1], arrival.at[c], peer),
        ]
        for copy in copies:
            copy.start()
        sums[c] = copies

    def pass_on(c):
        sums[c][0].wait_recv()
        outbox[c, 2] = (late_sum[c] + diagonal_in[c].astype(jnp.float32)).astype(jnp.bfloat16)
        peer = y_peer if c % 2 == 0 else x_peer
        arrival = y_in if c % 2 == 0 else x_in
        copy = send(outbox.at[c, 2], arrival.at[c], peer)
        copy.start()
        sums[c].append(copy)

    def project(*together):
        halves = []
        for c in together:
            sums[c][1].wait_recv()
            sums[c][2].wait_recv()
            update = own_sum[c] + x_in[c].astype(jnp.float32) + y_in[c].astype(jnp.float32)
            halves.append(patches_ref[c * part : (c + 1) * part, :].astype(jnp.float32) + update)
        if together[0] == 0:
            loads[2].wait()
            loads[3].wait()
        vision = jnp.concatenate(halves, axis=0).astype(jnp.bfloat16)
        for n in range(KV_HEADS // 2):
            columns = slice(n * pair, (n + 1) * pair)
            keys = jnp.dot(vision, key_map[:, columns], preferred_element_type=jnp.float32)
            values = jnp.dot(vision, value_map[:, columns], preferred_element_type=jnp.float32)
            for i in range(2):
                lanes = slice(i * HEAD_DIM, (i + 1) * HEAD_DIM)
                head_keys = root_rows(keys[:, lanes]).astype(jnp.bfloat16)
                head_values = values[:, lanes].astype(jnp.bfloat16)
                for t, c in enumerate(together):
                    span = slice(t * part, (t + 1) * part)
                    kv_box[c, 2 * n + i, :, 0:HEAD_DIM] = head_keys[span]
                    kv_box[c, 2 * n + i, :, HEAD_DIM:pair] = head_values[span]
        for c in together:
            kv_sends[c] = [
                send(kv_box.at[c, peer[1]], kv_all.at[c, dev], peer) for peer in dev_peers
            ]
            for copy in kv_sends[c]:
                copy.start()
            kv_all[c, dev] = kv_box[c, dev]

    def attend(c):
        for copy in kv_sends[c]:
            copy.wait_recv()
        keys = kv_all[c, :, :, 0:HEAD_DIM].reshape(devices * part, HEAD_DIM)
        values = kv_all[c, :, :, HEAD_DIM:pair].reshape(devices * part, HEAD_DIM)
        values = jnp.concatenate([values, jnp.ones_like(values)], axis=1)
        for g in range(4):
            scores = lax.dot_general(
                query_all[g], keys, (((1,), (1,)), ((), ())), preferred_element_type=jnp.float32
            )
            weights = jnp.exp2(scores * (HEAD_DIM ** (-0.5) * 1.4426950408889634)).reshape(
                heads, text_rows, devices * part
            ) * mask[c, g][None]
            added = jnp.dot(
                weights.reshape(heads * text_rows, devices * part).astype(jnp.bfloat16),
                values,
                preferred_element_type=jnp.float32,
            )
            gathered[g] = added if c == 0 else gathered[g] + added

    sums = [None] * chunks
    kv_sends = [None] * chunks
    loads[0].wait()
    loads[1].wait()
    arrive(0)
    feed_forward(0)
    forward(2)
    arrive(1)
    feed_forward(1)
    forward(3)
    pass_on(0)
    pass_on(1)
    arrive(2)
    feed_forward(2)
    project(0)
    arrive(3)
    feed_forward(3)
    pass_on(2)
    project(1)
    pass_on(3)
    project(2)
    for copy in query_sends:
        copy.wait_recv()
    attend(0)
    project(3)
    attend(1)
    attend(2)
    attend(3)

    row = lax.broadcasted_iota(jnp.int32, (16, pair), 0)
    lane = lax.broadcasted_iota(jnp.int32, (16, pair), 1)
    pick = jnp.where((lane == row * HEAD_DIM) & (row < 2), 1.0, 0.0).astype(jnp.bfloat16)
    group_sends = []
    for k, peer in enumerate(pool_peers):
        group = peer[0]
        group_out[k] = gathered[group, :, 0:HEAD_DIM].astype(jnp.bfloat16)
        copy = send(group_out.at[k], group_in.at[k], peer)
        copy.start()
        group_sends.append(copy)
    for k, peer in enumerate(pool_peers):
        total = gathered[peer[0], :, HEAD_DIM:pair]
        coarse = total.astype(jnp.bfloat16)
        fine = (total - coarse.astype(jnp.float32)).astype(jnp.bfloat16)
        total_out[k] = lax.dot_general(
            pick,
            jnp.concatenate([coarse, fine], axis=1),
            (((1,), (1,)), ((), ())),
            preferred_element_type=jnp.float32,
        ).astype(jnp.bfloat16)
        copy = send(total_out.at[k], total_in.at[k], peer)
        copy.start()
        group_sends.append(copy)
    for copy in group_sends:
        copy.wait_recv()
    top = gathered[pool, :, 0:HEAD_DIM]
    for k in range(3):
        top = top + group_in[k].astype(jnp.float32)
    totals = jnp.concatenate([total_in[k] for k in range(3)], axis=0)
    total = gathered[pool, :, HEAD_DIM:pair] + lax.dot_general(
        totals,
        jnp.ones((totals.shape[0], HEAD_DIM), jnp.bfloat16),
        (((0,), (0,)), ((), ())),
        preferred_element_type=jnp.float32,
    )
    result = top / jnp.where(total > 0.0, total, 1.0)
    for h in range(heads):
        attended[:, h * HEAD_DIM : (h + 1) * HEAD_DIM] = result[
            h * text_rows : (h + 1) * text_rows, :
        ]
    left = attended[...].astype(jnp.bfloat16)
    half = width_out // 2

    def piece(k):
        out_loads[k].wait()
        product = jnp.dot(left, big_map[k], preferred_element_type=jnp.float32)
        return jnp.concatenate([product[:, :half], product[:, half:]], axis=0)

    handed = []
    for k in range(chips):
        pair_out[k] = piece(k).astype(jnp.bfloat16)
        copy = send(pair_out.at[k], pair_in.at[k], partner)
        copy.start()
        handed.append(copy)
    copies = []
    for k in range(chips):
        folded = piece(chips + k)
        handed[k].wait_recv()
        folded = folded + pair_in[k].astype(jnp.float32)
        if k < chips - 1:
            piece_out[k] = folded.astype(jnp.bfloat16)
            copy = send(piece_out.at[k], piece_in.at[k], (pool, targets[chips + k]))
            copy.start()
            copies.append(copy)
    for k, copy in enumerate(copies):
        copy.wait_recv()
        folded = folded + piece_in[k].astype(jnp.float32)
    own = pl.ds(pl.multiple_of(dev * width_out, width_out), width_out)
    summed = jnp.concatenate([folded[:text_rows], folded[text_rows:]], axis=1)
    mixed_ref[...] = (text_raw[:, own] + summed).astype(jnp.bfloat16)
    for copy in everything:
        copy.wait_send()


def fused_body(
    patches,
    enc_tiles,
    req_tiles,
    req_owner,
    fc1_weight,
    fc2_weight,
    key_weight,
    value_weight,
    query_weight,
    out_weight,
    text_hidden,
):
    capacity, quarter, width = patches.shape
    slots, steps, model_width = text_hidden.shape
    groups, devices = lax.axis_size("pool"), lax.axis_size("dev")
    local = query_weight.shape[1]
    heads = local // HEAD_DIM
    chunks = 4
    count = capacity * quarter
    part = count // chunks
    text_rows = slots * steps
    vmem = pl.BlockSpec(memory_space=pltpu.VMEM)
    smem = pl.BlockSpec(memory_space=pltpu.SMEM)
    anywhere = pl.BlockSpec(memory_space=pl.ANY)
    bf16, f32 = jnp.bfloat16, jnp.float32
    width_out = model_width // devices
    pieces = model_width // width_out
    copies = 6 * chunks + 3 * (groups - 1) + (chunks + 1) * (devices - 1)
    group_box = (groups - 1, heads * text_rows, HEAD_DIM)
    total_box = (groups - 1, 16, heads * text_rows)
    piece = (2 * text_rows, width_out // 2)
    mixed = pl.pallas_call(
        block_kernel,
        out_shape=jax.ShapeDtypeStruct((text_rows, width_out), bf16),
        in_specs=[smem] * 3 + [vmem] * 2 + [anywhere] * 6,
        out_specs=vmem,
        scratch_shapes=[
            pltpu.VMEM(fc1_weight.shape, bf16),
            pltpu.VMEM(fc2_weight.shape, bf16),
            pltpu.VMEM(key_weight.shape, bf16),
            pltpu.VMEM(value_weight.shape, bf16),
            pltpu.VMEM((pieces, local, width_out), bf16),
            pltpu.VMEM((chunks, 4 * part, width), bf16),
            pltpu.VMEM((4 * part, fc1_weight.shape[1]), bf16),
            pltpu.VMEM((chunks, part, width), f32),
            pltpu.VMEM((chunks, part, width), f32),
            pltpu.VMEM((chunks, 3, part, width), bf16),
            pltpu.VMEM((chunks, part, width), bf16),
            pltpu.VMEM((chunks, part, width), bf16),
            pltpu.VMEM((chunks, part, width), bf16),
            pltpu.VMEM((chunks, KV_HEADS, part, 2 * HEAD_DIM), bf16),
            pltpu.VMEM((chunks, devices, part, 2 * HEAD_DIM), bf16),
            pltpu.VMEM((text_rows, model_width), f32),
            pltpu.VMEM((text_rows, model_width), f32),
            pltpu.VMEM((text_rows, local), f32),
            pltpu.VMEM((heads * text_rows, HEAD_DIM), f32),
            pltpu.VMEM((groups, heads * text_rows, HEAD_DIM), bf16),
            pltpu.VMEM((chunks, groups, text_rows, devices * part), f32),
            pltpu.VMEM((groups, heads * text_rows, 2 * HEAD_DIM), f32),
            pltpu.VMEM(group_box, bf16),
            pltpu.VMEM(group_box, bf16),
            pltpu.VMEM(total_box, bf16),
            pltpu.VMEM(total_box, bf16),
            pltpu.VMEM((text_rows, local), f32),
            pltpu.VMEM((devices // 2,) + piece, bf16),
            pltpu.VMEM((devices // 2,) + piece, bf16),
            pltpu.VMEM((devices // 2 - 1,) + piece, bf16),
            pltpu.VMEM((devices // 2 - 1,) + piece, bf16),
            pltpu.SemaphoreType.DMA((4 + pieces + devices,)),
            pltpu.SemaphoreType.DMA((copies,)),
            pltpu.SemaphoreType.DMA((copies,)),
        ],
        compiler_params=pltpu.CompilerParams(
            collective_id=0, has_side_effects=True, vmem_limit_bytes=58 * 1024 * 1024
        ),
        name="block",
    )(
        enc_tiles,
        req_tiles,
        req_owner.reshape(-1),
        patches.reshape(count, width),
        text_hidden,
        fc1_weight,
        fc2_weight,
        key_weight,
        value_weight,
        query_weight,
        out_weight,
    )
    return mixed.reshape(slots, steps, width_out)


def solution(mesh):
    fits = mesh.shape["pool"] == 4 and mesh.shape["dev"] == KV_HEADS
    return jax.shard_map(
        fused_body if fits else body,
        mesh=mesh,
        in_specs=(
            P("dev", "pool", None),
            P(),
            P(),
            P(),
            P(None, "pool"),
            P("pool", None),
            P(),
            P(),
            P(None, "dev"),
            P("dev", None),
            P("pool", None, None),
        ),
        out_specs=P("pool", None, "dev"),
        check_vma=False,
    )
```

```python
import jax
import jax.numpy as jnp
from jax import lax
from jax.experimental import pallas as pl
from jax.experimental.pallas import tpu as pltpu
from jax.sharding import PartitionSpec as P

MESH = pl.DeviceIdType.MESH

HEADS = 64
KV_HEADS = 8
HEAD_DIM = 128
MAXT = 4


epsilon = 1e-05


def layer_stats(values_in):
    center = values_in - jnp.mean(values_in, axis=-1, keepdims=True)
    spread = jnp.mean(center * center, axis=-1, keepdims=True)
    return center / jnp.sqrt(spread + epsilon)


def rms_scale(values_in):
    return values_in / jnp.sqrt(jnp.mean(values_in * values_in, axis=-1, keepdims=True) + epsilon)


def slot_tables(enc_tiles, req_tiles, req_owner, groups, slots, capacity, most_tiles):
    enc_start = jnp.cumsum(enc_tiles) - enc_tiles
    req_start = jnp.cumsum(req_tiles) - req_tiles
    owner = req_owner[:, 0]
    group_ids = jnp.arange(groups, dtype=jnp.int32)
    member = (owner[:, None] == group_ids[None, :]).astype(jnp.int32)
    rank_in = jnp.sum((jnp.cumsum(member, axis=0) - 1) * member, axis=1)
    slot_ids = jnp.arange(slots, dtype=jnp.int32)
    match = (
        (owner[None, None, :] == group_ids[:, None, None])
        & (rank_in[None, None, :] == slot_ids[None, :, None])
    ).astype(jnp.int32)
    live = jnp.sum(match, axis=2) > 0
    length = jnp.sum(match * req_tiles[None, None, :], axis=2)
    first_tile = jnp.sum(match * req_start[None, None, :], axis=2)
    position = jnp.arange(most_tiles, dtype=jnp.int32)
    valid = position[None, None, :] < length[:, :, None]
    tile_index = first_tile[:, :, None] + position[None, None, :]
    column = jnp.sum((enc_start <= tile_index[..., None]).astype(jnp.int32), axis=-1) - 1
    column_hit = (column[..., None] == jnp.arange(enc_tiles.shape[0], dtype=jnp.int32)).astype(
        jnp.int32
    )
    column_start = jnp.sum(column_hit * enc_start, axis=-1)
    source = column * capacity + tile_index - column_start
    source = jnp.where(valid, source, 0)
    return (source, valid, live)


def place_tiles(received, source, valid):
    flat_rows = received.reshape((received.shape[0] * received.shape[1],) + received.shape[2:])
    picked = jnp.take(flat_rows, source.reshape(-1), axis=0)
    picked = picked.reshape(source.shape + flat_rows.shape[1:])
    return jnp.where(valid[..., None, None], picked, jnp.zeros_like(picked))


def body(
    patches,
    enc_tiles,
    req_tiles,
    req_owner,
    fc1_weight,
    fc2_weight,
    key_weight,
    value_weight,
    query_weight,
    out_weight,
    text_hidden,
):
    capacity, quarter, width_in = patches.shape
    groups = lax.axis_size("pool")
    devices = lax.axis_size("dev")
    share_count = devices // KV_HEADS
    local_heads = HEADS // devices
    slots, steps, model_width = text_hidden.shape
    flat_patches = patches.reshape(capacity * quarter, width_in)
    normed = layer_stats(flat_patches.astype(jnp.float32)).astype(jnp.bfloat16)
    widened = jax.nn.gelu(
        jnp.dot(
            lax.all_gather(normed, "pool", axis=0, tiled=True),
            fc1_weight,
            preferred_element_type=jnp.float32,
        ),
        approximate=False,
    ).astype(jnp.bfloat16)
    update = lax.psum_scatter(
        jnp.dot(widened, fc2_weight, preferred_element_type=jnp.float32),
        "pool",
        scatter_dimension=0,
        tiled=True,
    )
    vision = (flat_patches.astype(jnp.float32) + update).astype(jnp.bfloat16)
    key_rows = rms_scale(
        jnp.dot(vision, key_weight, preferred_element_type=jnp.float32).reshape(
            capacity * quarter, KV_HEADS, HEAD_DIM
        )
    ).astype(jnp.bfloat16)
    value_rows = (
        jnp.dot(vision, value_weight, preferred_element_type=jnp.float32)
        .astype(jnp.bfloat16)
        .reshape(capacity * quarter, KV_HEADS, HEAD_DIM)
    )
    paired_rows = jnp.concatenate([key_rows, value_rows], axis=-1).reshape(
        capacity, quarter, KV_HEADS, 2 * HEAD_DIM
    )
    heads_first = jnp.transpose(paired_rows, (2, 0, 1, 3))
    source, valid, live = slot_tables(
        enc_tiles, req_tiles, req_owner, groups, slots, capacity, MAXT
    )
    copies_out = jnp.repeat(heads_first, share_count, axis=0)
    received = lax.all_to_all(copies_out, "dev", split_axis=0, concat_axis=0, tiled=True)
    arrived = lax.all_to_all(
        place_tiles(received, source, valid), "pool", split_axis=0, concat_axis=0, tiled=True
    )
    group_index = lax.axis_index("pool")
    slot_valid = lax.dynamic_index_in_dim(valid, group_index, 0, keepdims=False).astype(jnp.float32)
    slot_live = lax.dynamic_index_in_dim(live, group_index, 0, keepdims=False)
    normed_text = (
        rms_scale(text_hidden.astype(jnp.float32))
        .astype(jnp.bfloat16)
        .reshape(slots * steps, model_width)
    )
    query = jnp.dot(normed_text, query_weight, preferred_element_type=jnp.float32).reshape(
        slots, steps * local_heads, HEAD_DIM
    )
    query = rms_scale(query).astype(jnp.bfloat16)
    scores = jnp.einsum(
        "rad,prmnd->rapmn", query, arrived[..., :HEAD_DIM], preferred_element_type=jnp.float32
    ) * HEAD_DIM ** (-0.5)
    weights = jnp.exp(scores) * slot_valid[:, None, None, :, None]
    total = jnp.sum(weights, axis=(2, 3, 4))
    total = jnp.where(slot_live[:, None], total, jnp.ones_like(total))
    weights = (weights / total[:, :, None, None, None]).astype(jnp.bfloat16)
    attended = jnp.einsum(
        "rapmn,prmnd->rad", weights, arrived[..., HEAD_DIM:], preferred_element_type=jnp.float32
    ).astype(jnp.bfloat16)
    partial_out = jnp.dot(
        attended.reshape(slots * steps, local_heads * HEAD_DIM),
        out_weight,
        preferred_element_type=jnp.float32,
    )
    summed = lax.psum_scatter(
        partial_out.astype(jnp.bfloat16), "dev", scatter_dimension=1, tiled=True
    ).astype(jnp.float32)
    width_out = model_width // devices
    residual = lax.dynamic_slice_in_dim(
        text_hidden, lax.axis_index("dev") * width_out, width_out, 2
    )
    mixed = (residual.reshape(slots * steps, width_out).astype(jnp.float32) + summed).astype(
        jnp.bfloat16
    )
    return mixed.reshape(slots, steps, width_out)


def center_rows(values_in):
    center = values_in - jnp.mean(values_in, axis=-1, keepdims=True)
    return center * lax.rsqrt(jnp.mean(center * center, axis=-1, keepdims=True) + epsilon)


def root_rows(values_in):
    return values_in * lax.rsqrt(
        jnp.mean(values_in * values_in, axis=-1, keepdims=True) + epsilon
    )


def remote(source, target, send_sems, recv_sems, index, device):
    return pltpu.make_async_remote_copy(
        src_ref=source,
        dst_ref=target,
        send_sem=send_sems.at[index],
        recv_sem=recv_sems.at[index],
        device_id=device,
        device_id_type=MESH,
    )


def greet(pool_peers, dev_peers):
    barrier = pltpu.get_barrier_semaphore()
    for peer in pool_peers + dev_peers:
        pl.semaphore_signal(barrier, inc=1, device_id=peer, device_id_type=MESH)
    pl.semaphore_wait(barrier, len(pool_peers) + len(dev_peers))


def block_kernel(
    enc_ref,
    tiles_ref,
    owner_ref,
    patches_ref,
    text_ref,
    fc1_hbm,
    fc2_hbm,
    key_hbm,
    value_hbm,
    query_hbm,
    out_hbm,
    mixed_ref,
    fc1,
    fc2,
    key_map,
    value_map,
    big_map,
    rows,
    hidden,
    own_sum,
    late_sum,
    outbox,
    diagonal_in,
    x_in,
    y_in,
    kv_box,
    kv_all,
    text_raw,
    text_normed,
    query_sum,
    query_flat,
    query_all,
    mask,
    gathered,
    group_out,
    group_in,
    total_out,
    total_in,
    attended,
    pair_out,
    pair_in,
    piece_out,
    piece_in,
    local_sems,
    send_sems,
    recv_sems,
):
    pool, dev = lax.axis_index("pool"), lax.axis_index("dev")
    x, y = lax.rem(pool, 2), lax.div(pool, 2)
    x_peer = (y * 2 + 1 - x, dev)
    y_peer = ((1 - y) * 2 + x, dev)
    devices = kv_all.shape[1]
    chunks = rows.shape[0]
    part = rows.shape[1] // 4
    width = rows.shape[2]
    tile = 256
    slots, steps = text_ref.shape[0], text_ref.shape[1]
    text_rows = slots * steps
    pieces, depth, width_out = big_map.shape
    heads = query_sum.shape[1] // HEAD_DIM
    pair = 2 * HEAD_DIM
    tile_slots = 8

    loads = [
        pltpu.make_async_copy(fc1_hbm, fc1, local_sems.at[0]),
        pltpu.make_async_copy(fc2_hbm, fc2, local_sems.at[1]),
        pltpu.make_async_copy(key_hbm, key_map, local_sems.at[2]),
        pltpu.make_async_copy(value_hbm, value_map, local_sems.at[3]),
    ]
    query_loads = [
        pltpu.make_async_copy(
            query_hbm.at[pl.ds(k * depth, depth), :], big_map.at[k], local_sems.at[4 + k]
        )
        for k in range(pieces)
    ]
    chips = devices // 2
    chip, core = lax.div(dev, 2), lax.rem(dev, 2)
    ahead = [lax.rem(chip + k, chips) for k in list(range(1, chips)) + [0]]
    targets = [place * 2 + 1 - core for place in ahead] + [place * 2 + core for place in ahead]
    partner = (pool, chip * 2 + 1 - core)
    out_loads = [
        pltpu.make_async_copy(
            out_hbm.at[:, pl.ds(pl.multiple_of(target * width_out, width_out), width_out)],
            big_map.at[k],
            local_sems.at[4 + pieces + k],
        )
        for k, target in enumerate(targets)
    ]
    for load in query_loads[:3] + loads[:2] + query_loads[3:] + loads[2:]:
        load.start()

    pool_peers = [(lax.rem(pool + k, 4), dev) for k in range(1, 4)]
    dev_peers = [(pool, lax.rem(dev + k, devices)) for k in range(1, devices)]

    def normalize(c):
        values = patches_ref[c * part : (c + 1) * part, :].astype(jnp.float32)
        rows[c, 0:part, :] = center_rows(values).astype(jnp.bfloat16)

    normalize(0)
    greet(pool_peers, dev_peers)

    count = [0]
    everything = []

    def send(source, target, device):
        copy = remote(source, target, send_sems, recv_sems, count[0], device)
        count[0] += 1
        everything.append(copy)
        return copy

    def block(c, k):
        return rows.at[c, pl.ds(k * part, part)]

    to_x = [send(block(c, 0), block(c, 1), x_peer) for c in range(chunks)]
    to_y = [send(block(c, 0), block(c, 2), y_peer) for c in range(chunks)]
    onward = [
        send(block(c, 1), block(c, 3), y_peer)
        if c % 2 == 0
        else send(block(c, 2), block(c, 3), x_peer)
        for c in range(chunks)
    ]

    def forward(c):
        first = to_x[c] if c % 2 == 0 else to_y[c]
        first.wait_recv()
        onward[c].start()

    def arrive(c):
        second = to_y[c] if c % 2 == 0 else to_x[c]
        second.wait_recv()
        onward[c].wait_recv()

    to_x[0].start()
    to_y[0].start()
    normalize(1)
    to_y[1].start()
    to_x[1].start()

    for s in range(slots):
        text_raw[s * steps : (s + 1) * steps, :] = text_ref[s].astype(jnp.float32)
    text_normed[...] = root_rows(text_raw[...])
    query_sum[...] = jnp.zeros_like(query_sum)

    def query_step(k):
        query_loads[k].wait()
        query_sum[...] += jnp.dot(
            text_normed[:, k * depth : (k + 1) * depth].astype(jnp.bfloat16),
            big_map[k],
            preferred_element_type=jnp.float32,
        )

    for c in range(2, chunks):
        normalize(c)
    query_step(0)
    query_step(1)
    forward(0)
    forward(1)
    for c in range(2, chunks):
        to_x[c].start()
        to_y[c].start()
    query_step(2)

    def finish_query():
        for load in out_loads:
            load.start()
        for h in range(heads):
            query_flat[h * text_rows : (h + 1) * text_rows, :] = root_rows(
                query_sum[:, h * HEAD_DIM : (h + 1) * HEAD_DIM]
            )
        query_all[pool] = query_flat[...].astype(jnp.bfloat16)
        for peer in pool_peers:
            copy = send(query_all.at[pool], query_all.at[pool], peer)
            copy.start()
            query_sends.append(copy)

    query_sends = []

    def tables():
        span = devices * part
        requests = tiles_ref.shape[0]
        quarter = part * chunks // tile_slots
        column = lax.broadcasted_iota(jnp.int32, (text_rows, span), 1)
        row_slot = lax.div(lax.broadcasted_iota(jnp.int32, (text_rows, span), 0), steps)
        source = lax.div(column, part)
        inner = lax.div(lax.rem(column, part), quarter)
        begin = jnp.zeros((text_rows, span), jnp.int32)
        size = jnp.zeros((text_rows, span), jnp.int32)
        running = 0
        for e in range(devices):
            begin = jnp.where(source == e, running, begin)
            size = jnp.where(source == e, enc_ref[e], size)
            running = running + enc_ref[e]
        owners = [owner_ref[r] for r in range(requests)]
        names, starts, ends = [], [], []
        running = 0
        for r in range(requests):
            rank = 0
            for earlier in range(r):
                rank = rank + jnp.where(owners[earlier] == owners[r], 1, 0)
            names.append(owners[r] * slots + rank)
            starts.append(running)
            running = running + tiles_ref[r]
            ends.append(running)
        for c in range(chunks):
            place = inner + c * (part // quarter)
            index = begin + place
            name = jnp.full((text_rows, span), -1, jnp.int32)
            for r in range(requests):
                name = jnp.where((index >= starts[r]) & (index < ends[r]), names[r], name)
            name = jnp.where(place < size, name, -1)
            for g in range(4):
                mask[c, g] = jnp.where(row_slot + g * slots == name, 1.0, 0.0)


    def feed_forward(c):
        for n in range(fc1.shape[1] // tile):
            columns = slice(n * tile, (n + 1) * tile)
            pre = jnp.dot(rows[c], fc1[:, columns], preferred_element_type=jnp.float32)
            hidden[:, columns] = (0.5 * pre * (1.0 + lax.erf(pre * 0.7071067811865476))).astype(
                jnp.bfloat16
            )
        late = 2 if c % 2 == 0 else 1
        early = 3 - late
        for n in range(width // tile):
            columns = slice(n * tile, (n + 1) * tile)
            product = jnp.dot(hidden[...], fc2[:, columns], preferred_element_type=jnp.float32)
            outbox[c, 0, :, columns] = product[3 * part : 4 * part, :].astype(jnp.bfloat16)
            outbox[c, 1, :, columns] = product[early * part : (early + 1) * part, :].astype(
                jnp.bfloat16
            )
            own_sum[c, :, columns] = product[0:part, :]
            late_sum[c, :, columns] = product[late * part : (late + 1) * part, :]
        peer = x_peer if c % 2 == 0 else y_peer
        arrival = x_in if c % 2 == 0 else y_in
        copies = [
            send(outbox.at[c, 0], diagonal_in.at[c], peer),
            send(outbox.at[c, 1], arrival.at[c], peer),
        ]
        for copy in copies:
            copy.start()
        sums[c] = copies

    def pass_on(c):
        sums[c][0].wait_recv()
        outbox[c, 2] = (late_sum[c] + diagonal_in[c].astype(jnp.float32)).astype(jnp.bfloat16)
        peer = y_peer if c % 2 == 0 else x_peer
        arrival = y_in if c % 2 == 0 else x_in
        copy = send(outbox.at[c, 2], arrival.at[c], peer)
        copy.start()
        sums[c].append(copy)

    def project(*together):
        halves = []
        for c in together:
            sums[c][1].wait_recv()
            sums[c][2].wait_recv()
            update = own_sum[c] + x_in[c].astype(jnp.float32) + y_in[c].astype(jnp.float32)
            halves.append(patches_ref[c * part : (c + 1) * part, :].astype(jnp.float32) + update)
        if together[0] == 0:
            loads[2].wait()
            loads[3].wait()
        vision = jnp.concatenate(halves, axis=0).astype(jnp.bfloat16)
        for n in range(KV_HEADS // 2):
            columns = slice(n * pair, (n + 1) * pair)
            keys = jnp.dot(vision, key_map[:, columns], preferred_element_type=jnp.float32)
            values = jnp.dot(vision, value_map[:, columns], preferred_element_type=jnp.float32)
            for i in range(2):
                lanes = slice(i * HEAD_DIM, (i + 1) * HEAD_DIM)
                head_keys = root_rows(keys[:, lanes]).astype(jnp.bfloat16)
                head_values = values[:, lanes].astype(jnp.bfloat16)
                for t, c in enumerate(together):
                    span = slice(t * part, (t + 1) * part)
                    kv_box[c, 2 * n + i, :, 0:HEAD_DIM] = head_keys[span]
                    kv_box[c, 2 * n + i, :, HEAD_DIM:pair] = head_values[span]
        for c in together:
            kv_sends[c] = [
                send(kv_box.at[c, peer[1]], kv_all.at[c, dev], peer) for peer in dev_peers
            ]
            for copy in kv_sends[c]:
                copy.start()
            kv_all[c, dev] = kv_box[c, dev]

    def attend(c):
        for copy in kv_sends[c]:
            copy.wait_recv()
        keys = kv_all[c, :, :, 0:HEAD_DIM].reshape(devices * part, HEAD_DIM)
        values = kv_all[c, :, :, HEAD_DIM:pair].reshape(devices * part, HEAD_DIM)
        values = jnp.concatenate([values, jnp.ones_like(values)], axis=1)
        for g in range(4):
            scores = lax.dot_general(
                query_all[g], keys, (((1,), (1,)), ((), ())), preferred_element_type=jnp.float32
            )
            weights = jnp.exp2(scores * (HEAD_DIM ** (-0.5) * 1.4426950408889634)).reshape(
                heads, text_rows, devices * part
            ) * mask[c, g][None]
            added = jnp.dot(
                weights.reshape(heads * text_rows, devices * part).astype(jnp.bfloat16),
                values,
                preferred_element_type=jnp.float32,
            )
            gathered[g] = added if c == 0 else gathered[g] + added

    sums = [None] * chunks
    kv_sends = [None] * chunks
    loads[0].wait()
    loads[1].wait()
    arrive(0)
    feed_forward(0)
    forward(2)
    arrive(1)
    feed_forward(1)
    forward(3)
    pass_on(0)
    pass_on(1)
    for k in range(3, 6):
        query_step(k)
    arrive(2)
    feed_forward(2)
    project(0)
    arrive(3)
    feed_forward(3)
    pass_on(2)
    project(1)
    pass_on(3)
    for k in range(6, pieces):
        query_step(k)
    finish_query()
    project(2)
    tables()
    for copy in query_sends:
        copy.wait_recv()
    attend(0)
    project(3)
    attend(1)
    attend(2)
    attend(3)

    row = lax.broadcasted_iota(jnp.int32, (16, pair), 0)
    lane = lax.broadcasted_iota(jnp.int32, (16, pair), 1)
    pick = jnp.where((lane == row * HEAD_DIM) & (row < 2), 1.0, 0.0).astype(jnp.bfloat16)
    group_sends = []
    for k, peer in enumerate(pool_peers):
        group = peer[0]
        group_out[k] = gathered[group, :, 0:HEAD_DIM].astype(jnp.bfloat16)
        copy = send(group_out.at[k], group_in.at[k], peer)
        copy.start()
        group_sends.append(copy)
    for k, peer in enumerate(pool_peers):
        total = gathered[peer[0], :, HEAD_DIM:pair]
        coarse = total.astype(jnp.bfloat16)
        fine = (total - coarse.astype(jnp.float32)).astype(jnp.bfloat16)
        total_out[k] = lax.dot_general(
            pick,
            jnp.concatenate([coarse, fine], axis=1),
            (((1,), (1,)), ((), ())),
            preferred_element_type=jnp.float32,
        ).astype(jnp.bfloat16)
        copy = send(total_out.at[k], total_in.at[k], peer)
        copy.start()
        group_sends.append(copy)
    for copy in group_sends:
        copy.wait_recv()
    top = gathered[pool, :, 0:HEAD_DIM]
    for k in range(3):
        top = top + group_in[k].astype(jnp.float32)
    totals = jnp.concatenate([total_in[k] for k in range(3)], axis=0)
    total = gathered[pool, :, HEAD_DIM:pair] + lax.dot_general(
        totals,
        jnp.ones((totals.shape[0], HEAD_DIM), jnp.bfloat16),
        (((0,), (0,)), ((), ())),
        preferred_element_type=jnp.float32,
    )
    result = top / jnp.where(total > 0.0, total, 1.0)
    for h in range(heads):
        attended[:, h * HEAD_DIM : (h + 1) * HEAD_DIM] = result[
            h * text_rows : (h + 1) * text_rows, :
        ]
    left = attended[...].astype(jnp.bfloat16)
    half = width_out // 2

    def piece(k):
        out_loads[k].wait()
        product = jnp.dot(left, big_map[k], preferred_element_type=jnp.float32)
        return jnp.concatenate([product[:, :half], product[:, half:]], axis=0)

    handed = []
    for k in range(chips):
        pair_out[k] = piece(k).astype(jnp.bfloat16)
        copy = send(pair_out.at[k], pair_in.at[k], partner)
        copy.start()
        handed.append(copy)
    copies = []
    for k in range(chips):
        folded = piece(chips + k)
        handed[k].wait_recv()
        folded = folded + pair_in[k].astype(jnp.float32)
        if k < chips - 1:
            piece_out[k] = folded.astype(jnp.bfloat16)
            copy = send(piece_out.at[k], piece_in.at[k], (pool, targets[chips + k]))
            copy.start()
            copies.append(copy)
    for k, copy in enumerate(copies):
        copy.wait_recv()
        folded = folded + piece_in[k].astype(jnp.float32)
    own = pl.ds(pl.multiple_of(dev * width_out, width_out), width_out)
    summed = jnp.concatenate([folded[:text_rows], folded[text_rows:]], axis=1)
    mixed_ref[...] = (text_raw[:, own] + summed).astype(jnp.bfloat16)
    for copy in everything:
        copy.wait_send()


def fused_body(
    patches,
    enc_tiles,
    req_tiles,
    req_owner,
    fc1_weight,
    fc2_weight,
    key_weight,
    value_weight,
    query_weight,
    out_weight,
    text_hidden,
):
    capacity, quarter, width = patches.shape
    slots, steps, model_width = text_hidden.shape
    groups, devices = lax.axis_size("pool"), lax.axis_size("dev")
    local = query_weight.shape[1]
    heads = local // HEAD_DIM
    chunks = 4
    count = capacity * quarter
    part = count // chunks
    text_rows = slots * steps
    vmem = pl.BlockSpec(memory_space=pltpu.VMEM)
    smem = pl.BlockSpec(memory_space=pltpu.SMEM)
    anywhere = pl.BlockSpec(memory_space=pl.ANY)
    bf16, f32 = jnp.bfloat16, jnp.float32
    width_out = model_width // devices
    pieces = model_width // width_out
    copies = 6 * chunks + 3 * (groups - 1) + (chunks + 1) * (devices - 1)
    group_box = (groups - 1, heads * text_rows, HEAD_DIM)
    total_box = (groups - 1, 16, heads * text_rows)
    piece = (2 * text_rows, width_out // 2)
    mixed = pl.pallas_call(
        block_kernel,
        out_shape=jax.ShapeDtypeStruct((text_rows, width_out), bf16),
        in_specs=[smem] * 3 + [vmem] * 2 + [anywhere] * 6,
        out_specs=vmem,
        scratch_shapes=[
            pltpu.VMEM(fc1_weight.shape, bf16),
            pltpu.VMEM(fc2_weight.shape, bf16),
            pltpu.VMEM(key_weight.shape, bf16),
            pltpu.VMEM(value_weight.shape, bf16),
            pltpu.VMEM((pieces, local, width_out), bf16),
            pltpu.VMEM((chunks, 4 * part, width), bf16),
            pltpu.VMEM((4 * part, fc1_weight.shape[1]), bf16),
            pltpu.VMEM((chunks, part, width), f32),
            pltpu.VMEM((chunks, part, width), f32),
            pltpu.VMEM((chunks, 3, part, width), bf16),
            pltpu.VMEM((chunks, part, width), bf16),
            pltpu.VMEM((chunks, part, width), bf16),
            pltpu.VMEM((chunks, part, width), bf16),
            pltpu.VMEM((chunks, KV_HEADS, part, 2 * HEAD_DIM), bf16),
            pltpu.VMEM((chunks, devices, part, 2 * HEAD_DIM), bf16),
            pltpu.VMEM((text_rows, model_width), f32),
            pltpu.VMEM((text_rows, model_width), f32),
            pltpu.VMEM((text_rows, local), f32),
            pltpu.VMEM((heads * text_rows, HEAD_DIM), f32),
            pltpu.VMEM((groups, heads * text_rows, HEAD_DIM), bf16),
            pltpu.VMEM((chunks, groups, text_rows, devices * part), f32),
            pltpu.VMEM((groups, heads * text_rows, 2 * HEAD_DIM), f32),
            pltpu.VMEM(group_box, bf16),
            pltpu.VMEM(group_box, bf16),
            pltpu.VMEM(total_box, bf16),
            pltpu.VMEM(total_box, bf16),
            pltpu.VMEM((text_rows, local), f32),
            pltpu.VMEM((devices // 2,) + piece, bf16),
            pltpu.VMEM((devices // 2,) + piece, bf16),
            pltpu.VMEM((devices // 2 - 1,) + piece, bf16),
            pltpu.VMEM((devices // 2 - 1,) + piece, bf16),
            pltpu.SemaphoreType.DMA((4 + pieces + devices,)),
            pltpu.SemaphoreType.DMA((copies,)),
            pltpu.SemaphoreType.DMA((copies,)),
        ],
        compiler_params=pltpu.CompilerParams(
            collective_id=0, has_side_effects=True, vmem_limit_bytes=58 * 1024 * 1024
        ),
        name="block",
    )(
        enc_tiles,
        req_tiles,
        req_owner.reshape(-1),
        patches.reshape(count, width),
        text_hidden,
        fc1_weight,
        fc2_weight,
        key_weight,
        value_weight,
        query_weight,
        out_weight,
    )
    return mixed.reshape(slots, steps, width_out)


def solution(mesh):
    fits = mesh.shape["pool"] == 4 and mesh.shape["dev"] == KV_HEADS
    return jax.shard_map(
        fused_body if fits else body,
        mesh=mesh,
        in_specs=(
            P("dev", "pool", None),
            P(),
            P(),
            P(),
            P(None, "pool"),
            P("pool", None),
            P(),
            P(),
            P(None, "dev"),
            P("dev", None),
            P("pool", None, None),
        ),
        out_specs=P("pool", None, "dev"),
        check_vma=False,
    )
```
